128 devices in a mesh: leaf: 64 (over z, y, x), front: 2 (over core).
Axes of the slice: x: 4, y: 4, z: 4, core: 2. Of those that a mesh axis runs over, the one named last changes fastest.
Arguments:
- rhs_parts: bfloat16 [64, 2, 1152, 256], P('leaf', 'front'), may hold values from -6 to 6
- send_order: int32 [64, 2, 1152], P('leaf', 'front'), may hold values from 0 to 1151, each once within a row
- recv_place: int32 [64, 2, 1152], P('leaf', 'front'), may hold values from 0 to 1151, each once within a row
- sep_rhs: bfloat16 [64, 2, 3, 16, 256], P('leaf', 'front'), may hold values from -6 to 6
- leaf_inv: bfloat16 [64, 2, 1152, 1152], P('leaf', 'front'), as said below
- leaf_panels: bfloat16 [64, 2, 3, 64, 1152], P('leaf', 'front'), may hold values from -0.1875 to 0.1875
- leaf_rows: int32 [64, 2, 3, 64], P('leaf', 'front'), may hold values from 0 to 255, as said below
- sep_inv: bfloat16 [64, 2, 32, 224], P('leaf', 'front'), as said below
- sep_panels: bfloat16 [64, 2, 3, 64, 16], P('leaf', 'front'), may hold values from -1.5 to 1.5
- sep_rows: int32 [64, 2, 3, 64], P('leaf', 'front'), may hold values from 0 to 255, as said below
Outputs:
- leaf_solution: float32 [64, 2, 1152, 256], P('leaf', 'front')
- sep_solution: bfloat16 [64, 2, 3, 16, 256], P('leaf', 'front')
The draws below stay inside these ranges and needn't reach their ends.
Inputs may be any that keep to these rules, and one draw needn't show every extreme that they name: Each block of leaf_inv is lower triangular with a positive diagonal. Each E_m[g] assembled from sep_inv is lower triangular with a positive diagonal. `leaf_rows`: within one device's block for level m the 64 row numbers are distinct, ascending and below S_m; each block holds row 0 and row S_m - 1. `sep_rows`: within one device's block for pair (m, k) the 64 row numbers are distinct, ascending and below S_k; each block holds row 0 and row S_k - 1.
All inputs are finite; a program needn't handle non-finite values.
Results may differ from the reference program's by a relative error of at most 0.018.
Values may be sent and summed in bfloat16 or wider, within the bound.
No kernel may reach another device: no remote copies, remote signals or barrier semaphores. Data moves between devices by JAX's collectives and lax.ppermute only.
A program may use at most 64 MiB of HBM per device.

```python
import math
import jax
import jax.numpy as jnp
from jax import lax

LEAF = 1152
NRHS = 256
SUB = 16
UPD = 64
LEVELS = 3
PAIRS = 3
N_LEAF = 64
N_FRONT = 2


def triangle_values(glob_row, glob_col, draw_low, draw_mid, order_sep):
    lower_part = jnp.where(glob_col < glob_row, 0.8 / math.sqrt(order_sep) * draw_low, 0.0)
    return lower_part + jnp.where(glob_col == glob_row, draw_mid, 0.0)


def rough_normal(key, dims_all):
    return jax.random.normal(key, dims_all, jnp.float32)


def draw_leaf_inv(key, part):
    key = jax.random.fold_in(key, 11)
    dims_all = (N_LEAF, N_FRONT, LEAF, LEAF)
    key_low, key_mid = jax.random.split(key)
    draw_low = rough_normal(key_low, dims_all)
    draw_mid = jax.random.uniform(key_mid, dims_all, jnp.float32, 0.6, 1.6)
    row_ids = lax.broadcasted_iota(jnp.int32, dims_all, 2)
    col_ids = lax.broadcasted_iota(jnp.int32, dims_all, 3)
    return triangle_values(row_ids, col_ids, draw_low, draw_mid, LEAF).astype(jnp.bfloat16)


def draw_sep_inv(key, part):
    key = jax.random.fold_in(key, 17)
    dims_all = (N_LEAF, N_FRONT, SUB * N_FRONT, SUB * (2 ** (LEVELS + 1) - 2))
    key_low, key_mid = jax.random.split(key)
    draw_low = rough_normal(key_low, dims_all)
    draw_mid = jax.random.uniform(key_mid, dims_all, jnp.float32, 0.6, 1.6)
    owner_ids = lax.broadcasted_iota(jnp.int32, dims_all, 0)
    front_ids = lax.broadcasted_iota(jnp.int32, dims_all, 1)
    inner_ids = lax.broadcasted_iota(jnp.int32, dims_all, 2)
    column_ids = lax.broadcasted_iota(jnp.int32, dims_all, 3)
    values = jnp.zeros(dims_all, jnp.float32)
    for height in range(LEVELS):
        group_span = 2 ** (height + 1)
        start_col = SUB * (group_span - 2)
        width_col = SUB * group_span
        glob_row = owner_ids % group_span * (SUB * N_FRONT) + inner_ids
        glob_col = front_ids * width_col + (column_ids - start_col)
        inside = (column_ids >= start_col) & (column_ids < start_col + width_col)
        values = jnp.where(inside, triangle_values(glob_row, glob_col, draw_low, draw_mid, group_span * SUB * N_FRONT), values)
    return values.astype(jnp.bfloat16)


def subset_rows(key_one, row_limit):
    inner = jax.random.permutation(key_one, row_limit - 2)[:UPD - 2].astype(jnp.int32) + 1
    first = jnp.zeros((1,), jnp.int32)
    last = jnp.full((1,), row_limit - 1, jnp.int32)
    return jnp.sort(jnp.concatenate([first, inner, last])).astype(jnp.int32)


def rows_for_limits(key, limits):
    stacked = []
    for index_one, row_limit in enumerate(limits):
        key_list = jax.random.split(jax.random.fold_in(key, index_one), N_LEAF * N_FRONT)
        stacked.append(jax.vmap(lambda key_one: subset_rows(key_one, row_limit))(key_list))
    return jnp.stack(stacked, axis=1).reshape(N_LEAF, N_FRONT, len(limits), UPD)


def draw_leaf_rows(key, part):
    key = jax.random.fold_in(key, 23)
    limits = [SUB * N_FRONT * 2 ** (height + 1) for height in range(LEVELS)]
    return rows_for_limits(key, limits)


def draw_sep_rows(key, part):
    key = jax.random.fold_in(key, 29)
    limits = []
    for lower_lvl in range(LEVELS):
        for upper_lvl in range(lower_lvl + 1, LEVELS):
            limits.append(SUB * N_FRONT * 2 ** (upper_lvl + 1))
    return rows_for_limits(key, limits)


def block_levels(key, dims, cuts, low, top_value):
    loudness, own = 1.0, jax.random.fold_in(key, 6)
    for axis_at, blocks in cuts:
        draws = jnp.exp(jax.random.uniform(jax.random.fold_in(own, axis_at), (blocks,), jnp.float32, low / len(cuts), top_value / len(cuts)))
        loudness = loudness * jnp.repeat(draws, dims[axis_at] // blocks).reshape([-1 if axis == axis_at else 1 for axis in range(len(dims))])
    return loudness


def noise(own_key, extent, deviation, most, cuts=(), kind=jnp.bfloat16):
    factor_of = block_levels(own_key, extent, cuts, -0.22, 0.18) if cuts else 1.0
    result = jax.random.normal(own_key, extent, jnp.float32) * deviation * factor_of
    return jnp.minimum(jnp.maximum(result, -most), most).astype(kind)


def setup_inputs(seed: int = 0) -> dict:
    arg_keys = jax.random.split(jax.random.key(seed), 11)
    rhs_parts = noise(arg_keys[0], (N_LEAF, N_FRONT, LEAF, NRHS), 1.0, 6.0, ((0, 64), (1, 2)))
    send_order = jax.vmap(lambda own: jax.random.permutation(own, LEAF))(jax.random.split(arg_keys[1], N_LEAF * N_FRONT)).reshape((N_LEAF, N_FRONT, LEAF)).astype(jnp.int32)
    recv_place = jax.vmap(lambda own: jax.random.permutation(own, LEAF))(jax.random.split(arg_keys[2], N_LEAF * N_FRONT)).reshape((N_LEAF, N_FRONT, LEAF)).astype(jnp.int32)
    sep_rhs = noise(arg_keys[3], (N_LEAF, N_FRONT, LEVELS, SUB, NRHS), 1.0, 6.0, ((0, 64), (1, 2)))
    leaf_inv = draw_leaf_inv(jax.random.fold_in(arg_keys[10], 71), 0)
    leaf_panels = noise(arg_keys[5], (N_LEAF, N_FRONT, LEVELS, UPD, LEAF), LEAF ** -0.5, 0.1875, ((0, 64), (1, 2)))
    leaf_rows = draw_leaf_rows(jax.random.fold_in(arg_keys[10], 71), 0)
    sep_inv = draw_sep_inv(jax.random.fold_in(arg_keys[10], 71), 0)
    sep_panels = noise(arg_keys[8], (N_LEAF, N_FRONT, PAIRS, UPD, SUB), SUB ** -0.5, 1.5, ((0, 64), (1, 2)))
    sep_rows = draw_sep_rows(jax.random.fold_in(arg_keys[10], 71), 0)
    return dict(rhs_parts=rhs_parts, send_order=send_order, recv_place=recv_place, sep_rhs=sep_rhs, leaf_inv=leaf_inv, leaf_panels=leaf_panels, leaf_rows=leaf_rows, sep_inv=sep_inv, sep_panels=sep_panels, sep_rows=sep_rows)


def ancestor_pairs():
    listing = []
    for lower_lvl in range(LEVELS):
        for upper_lvl in range(lower_lvl + 1, LEVELS):
            listing.append((lower_lvl, upper_lvl))
    return listing


def to_groups(slices, height):
    group_span = 2 ** (height + 1)
    return slices.reshape(N_LEAF // group_span, group_span * N_FRONT * SUB, slices.shape[-1])


def from_groups(whole, height):
    return whole.reshape(N_LEAF, N_FRONT, SUB, whole.shape[-1])


def full_factor(sep_inv, height):
    group_span = 2 ** (height + 1)
    start_col = SUB * (group_span - 2)
    width_col = SUB * group_span
    pieces = sep_inv[:, :, :, start_col:start_col + width_col]
    pieces = pieces.reshape(N_LEAF // group_span, group_span, N_FRONT, SUB * N_FRONT, width_col)
    pieces = jnp.transpose(pieces, (0, 1, 3, 2, 4))
    return pieces.reshape(N_LEAF // group_span, group_span * SUB * N_FRONT, N_FRONT * width_col)


def group_ids(height):
    return jnp.arange(N_LEAF, dtype=jnp.int32) // (2 ** (height + 1))


def add_rows(totals, height, rows, values):
    owners = group_ids(height)
    return totals.at[owners[:, None, None], rows].add(values)


def pick_rows(whole, height, rows):
    owners = group_ids(height)
    return whole[owners[:, None, None], rows]


def reference(rhs_parts, send_order, recv_place, sep_rhs, leaf_inv, leaf_panels, leaf_rows, sep_inv, sep_panels, sep_rows):
    stretch_rows = LEAF // N_LEAF
    pair_list = ancestor_pairs()
    sent = jnp.take_along_axis(rhs_parts, send_order[..., None], axis=2)
    sent = sent.reshape(N_LEAF, N_FRONT, N_LEAF, stretch_rows, NRHS)
    received = jnp.transpose(sent, (2, 1, 0, 3, 4)).reshape(N_LEAF, N_FRONT, LEAF, NRHS)

    def place_rows(values, places):
        return jnp.zeros_like(values).at[places].set(values)

    owned_rows = jax.vmap(jax.vmap(place_rows))(received, recv_place)

    def forward_leaf(operands):
        inverse, column, panels = operands
        solved = jnp.dot(inverse, column, preferred_element_type=jnp.float32)
        rounded = solved.astype(jnp.bfloat16)
        pushes = jnp.stack([jnp.dot(panels[height], rounded, preferred_element_type=jnp.float32) for height in range(LEVELS)])
        return solved, pushes

    leaf_y, leaf_push = lax.map(forward_leaf, (leaf_inv.reshape(-1, LEAF, LEAF), owned_rows.reshape(-1, LEAF, NRHS), leaf_panels.reshape(-1, LEVELS, UPD, LEAF)))
    leaf_push = leaf_push.reshape(N_LEAF, N_FRONT, LEVELS, UPD, NRHS)

    totals = []
    for height in range(LEVELS):
        group_span = 2 ** (height + 1)
        order_sep = group_span * N_FRONT * SUB
        zeros_sum = jnp.zeros((N_LEAF // group_span, order_sep, NRHS), jnp.float32)
        totals.append(add_rows(zeros_sum, height, leaf_rows[:, :, height], leaf_push[:, :, height]))

    sep_y = []
    for height in range(LEVELS):
        right_side = to_groups(sep_rhs[:, :, height].astype(jnp.float32), height) - totals[height]
        rounded = lax.optimization_barrier(right_side.astype(jnp.bfloat16))
        factor = full_factor(sep_inv, height).astype(jnp.float32)
        solved = jnp.einsum("gij,gjr->gir", factor, rounded.astype(jnp.float32), precision=lax.Precision.HIGHEST)
        sep_y.append(solved)
        slices = lax.optimization_barrier(from_groups(solved.astype(jnp.bfloat16), height)).astype(jnp.float32)
        for pair_idx, (lower_lvl, upper_lvl) in enumerate(pair_list):
            if lower_lvl == height:
                values = jnp.einsum("ofus,ofsr->ofur", sep_panels[:, :, pair_idx].astype(jnp.float32), slices, precision=lax.Precision.HIGHEST)
                totals[upper_lvl] = add_rows(totals[upper_lvl], upper_lvl, sep_rows[:, :, pair_idx], values)

    sep_x = [None] * LEVELS
    for height in reversed(range(LEVELS)):
        y_slices = from_groups(sep_y[height], height)
        carried = jnp.zeros_like(y_slices)
        for pair_idx, (lower_lvl, upper_lvl) in enumerate(pair_list):
            if lower_lvl == height:
                picked = pick_rows(sep_x[upper_lvl], upper_lvl, sep_rows[:, :, pair_idx]).astype(jnp.float32)
                carried = carried + jnp.einsum("ofus,ofur->ofsr", sep_panels[:, :, pair_idx].astype(jnp.float32), picked, precision=lax.Precision.HIGHEST)
        residue = lax.optimization_barrier((y_slices - carried).astype(jnp.bfloat16))
        factor = full_factor(sep_inv, height).astype(jnp.float32)
        solved = jnp.einsum("gji,gjr->gir", factor, to_groups(residue, height).astype(jnp.float32), precision=lax.Precision.HIGHEST)
        sep_x[height] = solved.astype(jnp.bfloat16)

    picks = jnp.stack([pick_rows(sep_x[height], height, leaf_rows[:, :, height]) for height in range(LEVELS)], axis=2)

    def backward_leaf(operands):
        inverse, solved, panels, picked = operands
        carried = jnp.zeros((LEAF, NRHS), jnp.float32)
        for height in range(LEVELS):
            carried = carried + jnp.dot(panels[height].T, picked[height], preferred_element_type=jnp.float32)
        residue = (solved - carried).astype(jnp.bfloat16)
        return jnp.dot(inverse.T, residue, preferred_element_type=jnp.float32)

    leaf_solution = lax.map(backward_leaf, (leaf_inv.reshape(-1, LEAF, LEAF), leaf_y, leaf_panels.reshape(-1, LEVELS, UPD, LEAF), picks.reshape(-1, LEVELS, UPD, NRHS)))
    leaf_solution = leaf_solution.reshape(N_LEAF, N_FRONT, LEAF, NRHS)
    sep_solution = jnp.stack([from_groups(sep_x[height], height) for height in range(LEVELS)], axis=2)
    return leaf_solution, sep_solution
```

```python
import jax
import jax.numpy as jnp
import numpy as np
from jax import lax
from jax.experimental import pallas as pl
from jax.experimental.pallas import tpu as pltpu
from jax.sharding import Mesh, PartitionSpec as P

BF = jnp.bfloat16
F32 = jnp.float32
SUB = 16
TREE = 8
TEAM = 16
VMEM_CAP = 48 * 1024 * 1024

NN = (((1,), (0,)), ((), ()))
NT = (((1,), (1,)), ((), ()))


def dot(a, b, dims=NN):
    return lax.dot_general(a, b, dims, preferred_element_type=F32)


def lane_ids(rows, cols):
    return lax.broadcasted_iota(jnp.int32, (rows, cols), 1)


def row_ids(rows, cols):
    return lax.broadcasted_iota(jnp.int32, (rows, cols), 0)


def hot(mask):
    return jnp.where(mask, 1.0, 0.0).astype(BF)


def call(kernel, name, outs, scratch=(), flops=0, nbytes=0, smem_first=False, nargs=0):
    vmem = pl.BlockSpec(memory_space=pltpu.VMEM)
    specs = [vmem] * nargs
    if smem_first:
        specs[0] = pl.BlockSpec(memory_space=pltpu.SMEM)
    return pl.pallas_call(
        kernel,
        out_shape=outs,
        in_specs=specs,
        out_specs=jax.tree.map(lambda _: vmem, outs),
        scratch_shapes=list(scratch),
        compiler_params=pltpu.CompilerParams(vmem_limit_bytes=VMEM_CAP),
        cost_estimate=pl.CostEstimate(flops=flops, bytes_accessed=nbytes, transcendentals=0),
        name=name,
    )


def send_kernel(keep, pad, order_ref, rhs_ref, out_ref, picked_ref):
    rows, width = rhs_ref.shape
    rhs = rhs_ref[...]
    step = 384
    lanes = lane_ids(128, rows)
    for base in range(0, rows, step):
        blocks = []
        for at in range(base, base + step, 128):
            ids = jnp.broadcast_to(order_ref[:, at : at + 128], (128, 128)).T
            blocks.append(hot(jnp.concatenate([ids] * (rows // 128), axis=1) == lanes))
        picked_ref[base : base + step, :] = dot(jnp.concatenate(blocks, axis=0), rhs)
    tail = picked_ref.shape[0] - rows
    picked_ref[rows:, :] = jnp.zeros((tail, width), F32)
    for owner in range(rows // keep):
        out_ref[owner * pad : (owner + 1) * pad, :] = picked_ref[
            owner * keep : owner * keep + pad, :
        ].astype(BF)


def factor_kernel(
    place_ref, rows_ref, panels_ref, inv_ref, sinv_ref, span_ref, srow_ref,
    push_ref, back_ref, meta_ref, stage_ref,
):
    leaf = inv_ref.shape[0]
    slots = place_ref.shape[1]
    upd = rows_ref.shape[1]
    product = dot(panels_ref[...], inv_ref[...]).astype(BF)
    spread = hot(row_ids(leaf, slots) == place_ref[...])
    placed = dot(product, spread).astype(BF)
    for level, (base, order) in enumerate(((384, 64), (256, 128), (0, 256))):
        mine = hot(row_ids(order, upd) == rows_ref[level : level + 1, :])
        part = slice(level * upd, (level + 1) * upd)
        push_ref[base : base + order, :] = dot(mine, placed[part, :]).astype(BF)
        stage_ref[base : base + order, :] = dot(mine, product[part, :])
    push_ref[448:, :] = jnp.zeros((64, slots), BF)
    stage_ref[448:, :] = jnp.zeros((64, leaf), F32)
    back_ref[...] = stage_ref[...].T.astype(BF)
    cols = sinv_ref.shape[1]
    lane = lane_ids(cols, 256)
    source = jnp.where(
        lane < 128, lane + 96, jnp.where(lane < 192, lane - 96, jnp.where(lane < 224, lane - 192, -1))
    )
    meta_ref[0:32, :] = dot(sinv_ref[...], hot(row_ids(cols, 256) == source)).astype(BF)
    eye = hot(row_ids(SUB, SUB) == lane_ids(SUB, SUB))
    flipped = dot(eye, span_ref[...], NT)
    tail = jnp.concatenate(
        [srow_ref[...].astype(F32), jnp.zeros((SUB - srow_ref.shape[0], upd), F32)], axis=0
    )
    meta_ref[32:48, :] = jnp.concatenate([flipped, tail], axis=1).astype(BF)


def push_kernel(where_ref, recv_ref, push_ref, srhs_ref, meta_ref, out_ref, sum_ref):
    sum_ref[...] = -dot(push_ref[...], recv_ref[...])
    for level in range(3):
        at = pl.ds(pl.multiple_of(where_ref[level], SUB), SUB)
        sum_ref[at, :] = sum_ref[at, :] + srhs_ref[level].astype(F32)
    turned = sum_ref[...].T.astype(BF)
    meta = meta_ref[...]
    for member in range(TEAM):
        part = turned[member * SUB : (member + 1) * SUB, :]
        out_ref[member, 0:16, :] = part[:, 0:256]
        out_ref[member, 16:32, :] = part[:, 256:512]
        out_ref[member, 32:80, :] = meta


def leaf_kernel(place_ref, recv_ref, inv_ref, out_ref):
    leaf = inv_ref.shape[0]
    slots = place_ref.shape[1]
    spread = hot(row_ids(leaf, slots) == place_ref[...])
    owned = dot(spread, recv_ref[...])
    inv = inv_ref[...]
    y_t = dot(owned.T.astype(BF), inv, NT).astype(BF)
    out_ref[...] = dot(y_t, inv).T


def tree_kernel(got_ref, out_ref, e0_ref, e1_ref, e2_ref, a01_ref, a02_ref, a12_ref):
    lane = lane_ids(32, 128)
    none = jnp.zeros((32, 128), BF)
    for peer in range(TREE):
        rows = slice(peer * 32, (peer + 1) * 32)
        low0 = jnp.zeros((32, 128), F32)
        low1 = jnp.zeros((32, 128), F32)
        for front in range(2):
            src = peer * 2 + front
            e2_ref[rows, front * 128 : (front + 1) * 128] = got_ref[src, 32:64, 0:128]
            rest = got_ref[src, 32:64, 128:256].astype(F32)
            one = jnp.where(lane < 64, rest, 0.0)
            zero = jnp.where((lane >= 64) & (lane < 96), rest, 0.0)
            if front:
                one = pltpu.roll(one, 64, 1)
            to = ((peer // 2) % 2) * 64 + front * 32
            shift = (to - 64) % 128
            if shift:
                zero = pltpu.roll(zero, shift, 1)
            low1 = low1 + one
            low0 = low0 + zero
        for ref, low, tile in ((e1_ref, low1, peer // 4), (e0_ref, low0, peer // 4)):
            ref[rows, tile * 128 : (tile + 1) * 128] = low.astype(BF)
            ref[rows, (1 - tile) * 128 : (2 - tile) * 128] = none
    sub = row_ids(256, 64)
    for src in range(TEAM):
        half = src // 8 * 128
        for pair, ref in enumerate((a01_ref, a02_ref, a12_ref)):
            where = got_ref[src, 64 + pair : 65 + pair, 192:256].astype(F32).astype(jnp.int32)
            if pair == 0:
                where = where + half
            flipped = got_ref[src, 64:80, pair * 64 : (pair + 1) * 64]
            ref[src * SUB : (src + 1) * SUB, :] = dot(flipped, hot(sub == where), NT).astype(BF)
    r2 = jnp.zeros((SUB, 256), F32)
    for src in range(TEAM):
        r2 = r2 + got_ref[src, 0:16, :].astype(F32)
    tiles1, tiles0 = [], []
    lane = lane_ids(SUB, 128)
    for tile in range(2):
        total = jnp.zeros((SUB, 128), F32)
        for src in range(tile * 8, tile * 8 + 8):
            total = total + got_ref[src, 16:32, 0:128].astype(F32)
        tiles1.append(total)
        halves = []
        for group in range(2):
            total = jnp.zeros((SUB, 128), F32)
            for src in range(tile * 8 + group * 4, tile * 8 + group * 4 + 4):
                total = total + got_ref[src, 16:32, 128:256].astype(F32)
            halves.append(total)
        tiles0.append(jnp.where(lane < 64, halves[0], pltpu.roll(halves[1], 64, 1)))
    r1 = jnp.concatenate(tiles1, axis=1)
    r0 = jnp.concatenate(tiles0, axis=1)
    e0, e1, e2 = e0_ref[...], e1_ref[...], e2_ref[...]
    a01, a02, a12 = a01_ref[...], a02_ref[...], a12_ref[...]
    y0 = dot(r0.astype(BF), e0, NT)
    y0b = y0.astype(BF)
    y1 = dot((r1 - dot(y0b, a01)).astype(BF), e1, NT)
    y1b = y1.astype(BF)
    y2 = dot((r2 - dot(y0b, a02) - dot(y1b, a12)).astype(BF), e2, NT)
    x2 = dot(y2.astype(BF), e2).astype(BF)
    x1 = dot((y1 - dot(x2, a12, NT)).astype(BF), e1).astype(BF)
    x0 = dot((y0 - dot(x2, a02, NT) - dot(x1, a01, NT)).astype(BF), e0)
    low = jnp.where(lane < 64, 1.0, 0.0)
    for peer in range(TREE):
        tile = slice(peer // 4 * 128, peer // 4 * 128 + 128)
        own = x0[:, tile]
        if (peer // 2) % 2:
            own = pltpu.roll(own, 64, 1)
        own = (own * low).astype(BF)
        for front in range(2):
            dst = peer * 2 + front
            out_ref[dst, 0:16, :] = x2
            out_ref[dst, 16:32, 0:128] = x1[:, tile]
            out_ref[dst, 16:32, 128:256] = own


def finish_kernel(where_ref, got_ref, back_ref, leaf_ref, out_ref, sep_ref):
    high = got_ref[:, 0:16, :].reshape(256, 256)
    low = got_ref[:, 16:32, :].reshape(256, 256)
    out_ref[...] = (
        leaf_ref[...] - dot(back_ref[:, 0:256], high, NT) - dot(back_ref[:, 256:512], low, NT)
    )
    lane = lane_ids(SUB, 256)
    sub = row_ids(SUB, 256)
    for level, (base, table) in enumerate(((256, low), (256, low), (0, high))):
        pick = hot(lane == sub + (where_ref[level] - base))
        sep_ref[level] = dot(pick, table, NT).astype(BF)


def on_device(
    rhs_parts,
    send_order,
    recv_place,
    sep_rhs,
    leaf_inv,
    leaf_panels,
    leaf_rows,
    sep_inv,
    sep_panels,
    sep_rows,
):
    owners = lax.axis_size("tree") * lax.axis_size("peer")
    rhs = rhs_parts[0, 0]
    leaf, width = rhs.shape
    inv = leaf_inv[0, 0]
    panels = leaf_panels[0, 0].reshape(-1, leaf)
    keep = leaf // owners
    pad = -(-keep // 8) * 8
    slots = owners * pad
    sds = jax.ShapeDtypeStruct

    sent = call(
        lambda *refs: send_kernel(keep, pad, *refs),
        "send_rows",
        sds((slots, width), BF),
        [pltpu.VMEM((-(-(leaf - keep + pad) // 8) * 8 + 8, width), F32)],
        flops=2 * leaf * leaf * width,
        nbytes=2 * leaf * width * 2,
        nargs=2,
    )(send_order[0], rhs)
    recv = lax.all_to_all(
        sent.reshape(owners, pad, width), ("tree", "peer"), split_axis=0, concat_axis=0, tiled=True
    ).reshape(slots, width)

    place = jnp.pad(
        recv_place[0, 0].reshape(owners, keep), ((0, 0), (0, pad - keep)), constant_values=-1
    ).reshape(1, slots)
    push, back, meta = call(
        factor_kernel,
        "factor_products",
        (sds((512, slots), BF), sds((leaf, 512), BF), sds((48, 256), BF)),
        [pltpu.VMEM((512, leaf), F32)],
        flops=2 * 192 * leaf * (leaf + slots) + 2 * 448 * 64 * (leaf + slots),
        nbytes=2 * leaf * leaf + 4 * 512 * slots,
        nargs=7,
    )(
        place,
        leaf_rows[0, 0],
        panels,
        inv,
        sep_inv[0, 0],
        sep_panels[0, 0].reshape(-1, SUB),
        sep_rows[0, 0],
    )

    peer = lax.axis_index("peer")
    front = lax.axis_index("front")
    where = jnp.stack(
        [
            384 + (peer % 2 * 2 + front) * SUB,
            256 + (peer % 4 * 2 + front) * SUB,
            (peer * 2 + front) * SUB,
        ]
    ).astype(jnp.int32)
    team = ("peer", "front")
    chunks = call(
        push_kernel,
        "push_updates",
        sds((TEAM, 80, 256), BF),
        [pltpu.VMEM((512, width), F32)],
        flops=2 * 512 * slots * width,
        nbytes=2 * slots * (512 + width) + TEAM * 80 * 512,
        smem_first=True,
        nargs=5,
    )(where, recv, push, sep_rhs[0, 0], meta)
    got = lax.all_to_all(chunks, team, split_axis=0, concat_axis=0, tiled=True)

    bare = call(
        leaf_kernel,
        "leaf_solve",
        sds((leaf, width), F32),
        flops=2 * leaf * width * (2 * leaf + slots),
        nbytes=2 * leaf * leaf + 6 * slots * width,
        nargs=3,
    )(place, recv, inv)

    square = pltpu.VMEM((256, 256), BF)
    solved = call(
        tree_kernel,
        "separator_tree",
        sds((TEAM, 32, 256), BF),
        [square] * 6,
        flops=2 * 16 * 256 * 256 * 12 + 2 * 48 * 16 * 64 * 256,
        nbytes=TEAM * 112 * 512,
        nargs=1,
    )(got)
    back_got = lax.all_to_all(solved, team, split_axis=0, concat_axis=0, tiled=True)

    leaf_solution, sep_solution = call(
        finish_kernel,
        "finish",
        (sds((leaf, width), F32), sds((3, SUB, width), BF)),
        flops=2 * leaf * 512 * width,
        nbytes=leaf * width * 8 + leaf * 1024 + TEAM * 32 * 512,
        smem_first=True,
        nargs=4,
    )(where, back_got, back, bare)
    return leaf_solution[None, None], sep_solution[None, None]


def solution(mesh):
    leaves, fronts = mesh.shape["leaf"], mesh.shape["front"]
    grid = Mesh(
        np.asarray(mesh.devices).reshape(leaves // TREE, TREE, fronts), ("tree", "peer", "front")
    )
    leaf = ("tree", "peer")
    in_specs = (
        P(leaf, "front", None, None),
        P(leaf, "front", None),
        P(leaf, "front", None),
        P(leaf, "front", None, None, None),
        P(leaf, "front", None, None),
        P(leaf, "front", None, None, None),
        P(leaf, "front", None, None),
        P(leaf, "front", None, None),
        P(leaf, "front", None, None, None),
        P(leaf, "front", None, None),
    )
    out_specs = (P(leaf, "front", None, None), P(leaf, "front", None, None, None))
    return jax.shard_map(
        on_device, mesh=grid, in_specs=in_specs, out_specs=out_specs, check_vma=False
    )
```

```python
import jax
import jax.numpy as jnp
import numpy as np
from jax import lax
from jax.experimental import pallas as pl
from jax.experimental.pallas import tpu as pltpu
from jax.sharding import Mesh, PartitionSpec as P

BF = jnp.bfloat16
F32 = jnp.float32
SUB = 16
TREE = 8
TEAM = 16
VMEM_CAP = 40 * 1024 * 1024
VMEM_ALL = 62 * 1024 * 1024

NN = (((1,), (0,)), ((), ()))
NT = (((1,), (1,)), ((), ()))


def dot(a, b, dims=NN):
    return lax.dot_general(a, b, dims, preferred_element_type=F32)


def lane_ids(rows, cols):
    return lax.broadcasted_iota(jnp.int32, (rows, cols), 1)


def row_ids(rows, cols):
    return lax.broadcasted_iota(jnp.int32, (rows, cols), 0)


def hot(mask):
    return jnp.where(mask, 1.0, 0.0).astype(BF)


VM = pl.BlockSpec(memory_space=pltpu.VMEM)
SM = pl.BlockSpec(memory_space=pltpu.SMEM)
HB = pl.BlockSpec(memory_space=pltpu.HBM)
DMA = pltpu.SemaphoreType.DMA


def call(kernel, name, ins, outs, scratch=(), flops=0, nbytes=0, vmem=VMEM_CAP):
    return pl.pallas_call(
        kernel,
        out_shape=[shape for shape, _ in outs],
        in_specs=list(ins),
        out_specs=[spec for _, spec in outs],
        scratch_shapes=list(scratch),
        compiler_params=pltpu.CompilerParams(vmem_limit_bytes=vmem),
        cost_estimate=pl.CostEstimate(flops=flops, bytes_accessed=nbytes, transcendentals=0),
        name=name,
    )


def fetch(source, target, sem):
    copy = pltpu.make_async_copy(source, target, sem)
    copy.start()
    return copy


def send_kernel(keep, pad, order_hbm, rhs_hbm, out_hbm, order_ref, rhs_ref, picked_ref, out_ref, sems):
    rows, width = rhs_ref.shape
    order_in = fetch(order_hbm, order_ref, sems.at[0])
    rhs_in = fetch(rhs_hbm, rhs_ref, sems.at[1])
    tail = picked_ref.shape[0] - rows
    picked_ref[rows:, :] = jnp.zeros((tail, width), F32)
    owners = rows // keep
    step = 384
    lanes = lane_ids(128, rows)
    order_in.wait()
    hots = []
    for at in range(0, rows, 128):
        ids = jnp.broadcast_to(order_ref[:, at : at + 128], (128, 128)).T
        hots.append(hot(jnp.concatenate([ids] * (rows // 128), axis=1) == lanes))
    rhs_in.wait()
    rhs = rhs_ref[...]
    done = 0
    leaving = []
    for part in range(rows // step):
        block = jnp.concatenate(hots[part * 3 : part * 3 + 3], axis=0)
        picked_ref[part * step : (part + 1) * step, :] = dot(block, rhs)
        have = (part + 1) * step
        upto = owners if have == rows else ((have - pad) // keep + 1) // 2 * 2
        for owner in range(done, upto):
            out_ref[owner * pad : (owner + 1) * pad, :] = picked_ref[
                owner * keep : owner * keep + pad, :
            ].astype(BF)
        span = slice(done * pad, upto * pad)
        leaving.append(fetch(out_ref.at[span, :], out_hbm.at[span, :], sems.at[2 + part]))
        done = upto
    for copy in leaving:
        copy.wait()


def factor_kernel(
    where_ref, place_ref, rows_ref, srow_ref, panels_hbm, inv_hbm, sinv_hbm, span_hbm, srhs_hbm,
    push_ref, back_ref, side_ref, stage_ref, panels_ref, inv_ref, sinv_ref, span_ref, srhs_ref, sems,
):
    moves = [
        fetch(panels_hbm, panels_ref, sems.at[0]),
        fetch(inv_hbm, inv_ref, sems.at[1]),
        fetch(sinv_hbm, sinv_ref, sems.at[2]),
        fetch(span_hbm, span_ref, sems.at[3]),
        fetch(srhs_hbm, srhs_ref, sems.at[4]),
    ]
    leaf = inv_ref.shape[0]
    slots = place_ref.shape[1]
    upd = rows_ref.shape[1]
    spread = hot(row_ids(leaf, slots) == place_ref[...])
    push_ref[448:, :] = jnp.zeros((64, slots), BF)
    stage_ref[448:, :] = jnp.zeros((64, leaf), F32)
    for move in moves:
        move.wait()
    product = dot(panels_ref[...], inv_ref[...]).astype(BF)
    placed = dot(product, spread).astype(BF)
    for level, (base, order) in enumerate(((384, 64), (256, 128), (0, 256))):
        mine = hot(row_ids(order, upd) == rows_ref[level : level + 1, :])
        part = slice(level * upd, (level + 1) * upd)
        push_ref[base : base + order, :] = dot(mine, placed[part, :]).astype(BF)
        stage_ref[base : base + order, :] = dot(mine, product[part, :])
    back_ref[...] = stage_ref[...].T.astype(BF)
    cols = sinv_ref.shape[1]
    lane = lane_ids(cols, 256)
    source = jnp.where(
        lane < 128, lane + 96, jnp.where(lane < 192, lane - 96, jnp.where(lane < 224, lane - 192, -1))
    )
    side_ref[0:32, :] = dot(sinv_ref[...], hot(row_ids(cols, 256) == source)).astype(BF)
    tail = jnp.concatenate(
        [srow_ref[...].astype(F32), jnp.zeros((SUB - srow_ref.shape[0], upd), F32)], axis=0
    )
    flipped = [span_ref[pair].astype(F32) for pair in range(3)]
    side_ref[32:48, :] = jnp.concatenate(flipped + [tail], axis=1).astype(BF)
    side_ref[48:, :] = jnp.zeros((512, 256), BF)
    for level in range(3):
        at = pl.ds(pl.multiple_of(where_ref[level] + 48, SUB), SUB)
        side_ref[at, :] = srhs_ref[level]


def push_kernel(recv_ref, push_ref, side_ref, out_ref):
    sums = side_ref[48:, :].astype(F32) - dot(push_ref[...], recv_ref[...])
    turned = sums.T.astype(BF)
    meta = side_ref[0:48, :]
    for member in range(TEAM):
        part = turned[member * SUB : (member + 1) * SUB, :]
        out_ref[member, 0:16, :] = part[:, 0:256]
        out_ref[member, 16:32, :] = part[:, 256:512]
        out_ref[member, 32:80, :] = meta


def leaf_kernel(place_ref, recv_ref, inv_hbm, out_ref, inv_ref, sem):
    inv_in = fetch(inv_hbm, inv_ref, sem)
    leaf = inv_ref.shape[0]
    slots = place_ref.shape[1]
    spread = hot(row_ids(leaf, slots) == place_ref[...])
    owned = dot(spread, recv_ref[...]).T.astype(BF)
    inv_in.wait()
    inv = inv_ref[...]
    y_t = dot(owned, inv, NT).astype(BF)
    out_ref[...] = dot(y_t, inv).T


def tree_kernel(got_ref, bare_hbm, out_ref, e0_ref, e1_ref, e2_ref, a01_ref, a02_ref, a12_ref):
    lane = lane_ids(32, 128)
    none = jnp.zeros((32, 128), BF)
    for peer in range(TREE):
        rows = slice(peer * 32, (peer + 1) * 32)
        low0 = jnp.zeros((32, 128), F32)
        low1 = jnp.zeros((32, 128), F32)
        for front in range(2):
            src = peer * 2 + front
            e2_ref[rows, front * 128 : (front + 1) * 128] = got_ref[src, 32:64, 0:128]
            rest = got_ref[src, 32:64, 128:256].astype(F32)
            one = jnp.where(lane < 64, rest, 0.0)
            zero = jnp.where((lane >= 64) & (lane < 96), rest, 0.0)
            if front:
                one = pltpu.roll(one, 64, 1)
            to = ((peer // 2) % 2) * 64 + front * 32
            shift = (to - 64) % 128
            if shift:
                zero = pltpu.roll(zero, shift, 1)
            low1 = low1 + one
            low0 = low0 + zero
        for ref, low, tile in ((e1_ref, low1, peer // 4), (e0_ref, low0, peer // 4)):
            ref[rows, tile * 128 : (tile + 1) * 128] = low.astype(BF)
            ref[rows, (1 - tile) * 128 : (2 - tile) * 128] = none
    sub = row_ids(256, 64)
    for src in range(TEAM):
        half = src // 8 * 128
        for pair, ref in enumerate((a01_ref, a02_ref, a12_ref)):
            where = got_ref[src, 64 + pair : 65 + pair, 192:256].astype(F32).astype(jnp.int32)
            if pair == 0:
                where = where + half
            flipped = got_ref[src, 64:80, pair * 64 : (pair + 1) * 64]
            ref[src * SUB : (src + 1) * SUB, :] = dot(flipped, hot(sub == where), NT).astype(BF)
    r2 = jnp.zeros((SUB, 256), F32)
    for src in range(TEAM):
        r2 = r2 + got_ref[src, 0:16, :].astype(F32)
    tiles1, tiles0 = [], []
    lane = lane_ids(SUB, 128)
    for tile in range(2):
        total = jnp.zeros((SUB, 128), F32)
        for src in range(tile * 8, tile * 8 + 8):
            total = total + got_ref[src, 16:32, 0:128].astype(F32)
        tiles1.append(total)
        halves = []
        for group in range(2):
            total = jnp.zeros((SUB, 128), F32)
            for src in range(tile * 8 + group * 4, tile * 8 + group * 4 + 4):
                total = total + got_ref[src, 16:32, 128:256].astype(F32)
            halves.append(total)
        tiles0.append(jnp.where(lane < 64, halves[0], pltpu.roll(halves[1], 64, 1)))
    r1 = jnp.concatenate(tiles1, axis=1)
    r0 = jnp.concatenate(tiles0, axis=1)
    e0, e1, e2 = e0_ref[...], e1_ref[...], e2_ref[...]
    a01, a02, a12 = a01_ref[...], a02_ref[...], a12_ref[...]
    y0 = dot(r0.astype(BF), e0, NT)
    y0b = y0.astype(BF)
    y1 = dot((r1 - dot(y0b, a01)).astype(BF), e1, NT)
    y1b = y1.astype(BF)
    y2 = dot((r2 - dot(y0b, a02) - dot(y1b, a12)).astype(BF), e2, NT)
    x2 = dot(y2.astype(BF), e2).astype(BF)
    x1 = dot((y1 - dot(x2, a12, NT)).astype(BF), e1).astype(BF)
    x0 = dot((y0 - dot(x2, a02, NT) - dot(x1, a01, NT)).astype(BF), e0)
    low = jnp.where(lane < 64, 1.0, 0.0)
    for peer in range(TREE):
        tile = slice(peer // 4 * 128, peer // 4 * 128 + 128)
        own = x0[:, tile]
        if (peer // 2) % 2:
            own = pltpu.roll(own, 64, 1)
        own = (own * low).astype(BF)
        for front in range(2):
            dst = peer * 2 + front
            out_ref[dst, 0:16, :] = x2
            out_ref[dst, 16:32, 0:128] = x1[:, tile]
            out_ref[dst, 16:32, 128:256] = own


def finish_kernel(where_ref, got_ref, back_ref, leaf_ref, out_ref, sep_ref):
    high = got_ref[:, 0:16, :].reshape(256, 256)
    low = got_ref[:, 16:32, :].reshape(256, 256)
    out_ref[...] = (
        leaf_ref[...] - dot(back_ref[:, 0:256], high, NT) - dot(back_ref[:, 256:512], low, NT)
    )
    lane = lane_ids(SUB, 256)
    sub = row_ids(SUB, 256)
    for level, (base, table) in enumerate(((256, low), (256, low), (0, high))):
        pick = hot(lane == sub + (where_ref[level] - base))
        sep_ref[level] = dot(pick, table, NT).astype(BF)


def on_device(
    rhs_parts,
    send_order,
    recv_place,
    sep_rhs,
    leaf_inv,
    leaf_panels,
    leaf_rows,
    sep_inv,
    sep_panels,
    sep_rows,
):
    owners = lax.axis_size("tree") * lax.axis_size("peer")
    rhs = rhs_parts[0, 0]
    leaf, width = rhs.shape
    inv = leaf_inv[0, 0]
    panels = leaf_panels[0, 0].reshape(-1, leaf)
    keep = leaf // owners
    pad = -(-keep // 8) * 8
    slots = owners * pad
    sds = jax.ShapeDtypeStruct

    (sent,) = call(
        lambda *refs: send_kernel(keep, pad, *refs),
        "send_rows",
        [HB, HB],
        [(sds((slots, width), BF), HB)],
        [
            pltpu.VMEM((1, leaf), jnp.int32),
            pltpu.VMEM((leaf, width), BF),
            pltpu.VMEM((-(-(leaf - keep + pad) // 8) * 8 + 8, width), F32),
            pltpu.VMEM((slots, width), BF),
            DMA((5,)),
        ],
        flops=2 * leaf * leaf * width,
        nbytes=2 * leaf * width * 2,
        vmem=VMEM_ALL,
    )(send_order[0], rhs)
    recv = lax.all_to_all(
        sent.reshape(owners, pad, width), ("tree", "peer"), split_axis=0, concat_axis=0, tiled=True
    ).reshape(slots, width)

    place = jnp.pad(
        recv_place[0, 0].reshape(owners, keep), ((0, 0), (0, pad - keep)), constant_values=-1
    ).reshape(1, slots)
    peer = lax.axis_index("peer")
    front = lax.axis_index("front")
    where = jnp.stack(
        [
            384 + (peer % 2 * 2 + front) * SUB,
            256 + (peer % 4 * 2 + front) * SUB,
            (peer * 2 + front) * SUB,
        ]
    ).astype(jnp.int32)
    span = jnp.swapaxes(sep_panels[0, 0], 1, 2)
    push, back, side = call(
        factor_kernel,
        "factor_products",
        [SM, VM, VM, VM, HB, HB, HB, HB, HB],
        [(sds((512, slots), BF), VM), (sds((leaf, 512), BF), VM), (sds((560, 256), BF), VM)],
        [
            pltpu.VMEM((512, leaf), F32),
            pltpu.VMEM(panels.shape, BF),
            pltpu.VMEM((leaf, leaf), BF),
            pltpu.VMEM(sep_inv.shape[2:], BF),
            pltpu.VMEM(span.shape, BF),
            pltpu.VMEM(sep_rhs.shape[2:], BF),
            DMA((5,)),
        ],
        flops=2 * 192 * leaf * (leaf + slots) + 2 * 448 * 64 * (leaf + slots),
        nbytes=2 * leaf * leaf + 4 * 512 * slots,
    )(
        where,
        place,
        leaf_rows[0, 0],
        sep_rows[0, 0],
        panels,
        inv,
        sep_inv[0, 0],
        span,
        sep_rhs[0, 0],
    )

    team = ("peer", "front")
    (chunks,) = call(
        push_kernel,
        "push_updates",
        [VM, VM, VM],
        [(sds((TEAM, 80, 256), BF), VM)],
        flops=2 * 512 * slots * width,
        nbytes=2 * slots * (512 + width) + TEAM * 80 * 512,
    )(recv, push, side)
    got = lax.all_to_all(chunks, team, split_axis=0, concat_axis=0, tiled=True)

    (bare,) = call(
        leaf_kernel,
        "leaf_solve",
        [VM, VM, HB],
        [(sds((leaf, width), F32), VM)],
        [pltpu.VMEM((leaf, leaf), BF), DMA],
        flops=2 * leaf * width * (2 * leaf + slots),
        nbytes=2 * leaf * leaf + 6 * slots * width,
    )(place, recv, inv)

    square = pltpu.VMEM((256, 256), BF)
    (solved,) = call(
        tree_kernel,
        "separator_tree",
        [VM, pl.BlockSpec(memory_space=pl.ANY)],
        [(sds((TEAM, 32, 256), BF), VM)],
        [square] * 6,
        flops=2 * 16 * 256 * 256 * 12 + 2 * 48 * 16 * 64 * 256,
        nbytes=TEAM * 112 * 512,
    )(got, bare)
    back_got = lax.all_to_all(solved, team, split_axis=0, concat_axis=0, tiled=True)

    leaf_solution, sep_solution = call(
        finish_kernel,
        "finish",
        [SM, VM, VM, VM],
        [(sds((leaf, width), F32), VM), (sds((3, SUB, width), BF), VM)],
        flops=2 * leaf * 512 * width,
        nbytes=leaf * width * 8 + leaf * 1024 + TEAM * 32 * 512,
    )(where, back_got, back, bare)
    return leaf_solution[None, None], sep_solution[None, None]


def solution(mesh):
    leaves, fronts = mesh.shape["leaf"], mesh.shape["front"]
    grid = Mesh(
        np.asarray(mesh.devices).reshape(leaves // TREE, TREE, fronts), ("tree", "peer", "front")
    )
    leaf = ("tree", "peer")
    in_specs = (
        P(leaf, "front", None, None),
        P(leaf, "front", None),
        P(leaf, "front", None),
        P(leaf, "front", None, None, None),
        P(leaf, "front", None, None),
        P(leaf, "front", None, None, None),
        P(leaf, "front", None, None),
        P(leaf, "front", None, None),
        P(leaf, "front", None, None, None),
        P(leaf, "front", None, None),
    )
    out_specs = (P(leaf, "front", None, None), P(leaf, "front", None, None, None))
    return jax.shard_map(
        on_device, mesh=grid, in_specs=in_specs, out_specs=out_specs, check_vma=False
    )
```

```python
import jax
import jax.numpy as jnp
import numpy as np
from jax import lax
from jax.experimental import pallas as pl
from jax.experimental.pallas import tpu as pltpu
from jax.sharding import Mesh, PartitionSpec as P

BF = jnp.bfloat16
F32 = jnp.float32
SUB = 16
TREE = 8
TEAM = 16
VMEM_CAP = 40 * 1024 * 1024
VMEM_ALL = 62 * 1024 * 1024

NN = (((1,), (0,)), ((), ()))
NT = (((1,), (1,)), ((), ()))


def dot(a, b, dims=NN):
    return lax.dot_general(a, b, dims, preferred_element_type=F32)


def lane_ids(rows, cols):
    return lax.broadcasted_iota(jnp.int32, (rows, cols), 1)


def row_ids(rows, cols):
    return lax.broadcasted_iota(jnp.int32, (rows, cols), 0)


def hot(mask):
    return jnp.where(mask, 1.0, 0.0).astype(BF)


VM = pl.BlockSpec(memory_space=pltpu.VMEM)
SM = pl.BlockSpec(memory_space=pltpu.SMEM)
HB = pl.BlockSpec(memory_space=pltpu.HBM)
DMA = pltpu.SemaphoreType.DMA


def call(kernel, name, ins, outs, scratch=(), flops=0, nbytes=0, vmem=VMEM_CAP):
    return pl.pallas_call(
        kernel,
        out_shape=[shape for shape, _ in outs],
        in_specs=list(ins),
        out_specs=[spec for _, spec in outs],
        scratch_shapes=list(scratch),
        compiler_params=pltpu.CompilerParams(vmem_limit_bytes=vmem),
        cost_estimate=pl.CostEstimate(flops=flops, bytes_accessed=nbytes, transcendentals=0),
        name=name,
    )


def fetch(source, target, sem):
    copy = pltpu.make_async_copy(source, target, sem)
    copy.start()
    return copy


def send_kernel(keep, pad, order_hbm, rhs_hbm, out_hbm, order_ref, rhs_ref, picked_ref, out_ref, sems):
    rows, width = rhs_ref.shape
    order_in = fetch(order_hbm, order_ref, sems.at[0])
    rhs_in = fetch(rhs_hbm, rhs_ref, sems.at[1])
    tail = picked_ref.shape[0] - rows
    picked_ref[rows:, :] = jnp.zeros((tail, width), F32)
    owners = rows // keep
    step = 384
    lanes = lane_ids(128, rows)
    order_in.wait()
    hots = []
    for at in range(0, rows, 128):
        ids = jnp.broadcast_to(order_ref[:, at : at + 128], (128, 128)).T
        hots.append(hot(jnp.concatenate([ids] * (rows // 128), axis=1) == lanes))
    rhs_in.wait()
    rhs = rhs_ref[...]
    done = 0
    leaving = []
    for part in range(rows // step):
        block = jnp.concatenate(hots[part * 3 : part * 3 + 3], axis=0)
        picked_ref[part * step : (part + 1) * step, :] = dot(block, rhs)
        have = (part + 1) * step
        upto = owners if have == rows else ((have - pad) // keep + 1) // 2 * 2
        for owner in range(done, upto):
            out_ref[owner * pad : (owner + 1) * pad, :] = picked_ref[
                owner * keep : owner * keep + pad, :
            ].astype(BF)
        span = slice(done * pad, upto * pad)
        leaving.append(fetch(out_ref.at[span, :], out_hbm.at[span, :], sems.at[2 + part]))
        done = upto
    for copy in leaving:
        copy.wait()


def factor_kernel(
    place_ref, rows_ref, srow_ref, panels_hbm, inv_hbm, sinv_hbm, span_hbm, srhs_hbm,
    push_ref, back_ref, side_ref, panels_ref, inv_ref, sinv_ref, span_ref, srhs_ref, sems,
):
    moves = [
        fetch(sinv_hbm, sinv_ref, sems.at[0]),
        fetch(span_hbm, span_ref, sems.at[1]),
        fetch(srhs_hbm, srhs_ref, sems.at[2]),
        fetch(panels_hbm, panels_ref, sems.at[3]),
        fetch(inv_hbm, inv_ref, sems.at[4]),
    ]
    leaf = inv_ref.shape[0]
    slots = place_ref.shape[1]
    upd = rows_ref.shape[2]
    spread = hot(row_ids(leaf, slots) == place_ref[...])
    for move in moves:
        move.wait()
    product = dot(panels_ref[...], inv_ref[...])
    push_ref[...] = dot(product.astype(BF), spread).astype(BF)
    padded = jnp.concatenate([product, jnp.zeros((256 - product.shape[0], leaf), F32)], axis=0)
    back_ref[...] = padded.T.astype(BF)
    cols = sinv_ref.shape[1]
    lane = lane_ids(cols, 256)
    source = jnp.where(
        lane < 128, lane + 96, jnp.where(lane < 192, lane - 96, jnp.where(lane < 224, lane - 192, -1))
    )
    side_ref[0:32, :] = dot(sinv_ref[...], hot(row_ids(cols, 256) == source)).astype(BF)
    lists = [srow_ref[pair].astype(F32) for pair in range(3)]
    lists += [rows_ref[level].astype(F32) for level in range(3)]
    lists = jnp.concatenate(lists + [jnp.zeros((SUB - 6, upd), F32)], axis=0)
    flipped = [span_ref[pair].astype(F32) for pair in range(3)]
    side_ref[32:48, :] = jnp.concatenate(flipped + [lists], axis=1).astype(BF)
    for level in range(3):
        side_ref[48 + level * SUB : 64 + level * SUB, :] = srhs_ref[level]
    side_ref[96:112, :] = jnp.zeros((SUB, 256), BF)


def push_kernel(recv_ref, push_ref, side_ref, out_ref):
    sums = dot(push_ref[...], recv_ref[...])
    rows = jnp.concatenate([sums, side_ref[48:112, :].astype(F32)], axis=0)
    turned = rows.T.astype(BF)
    meta = side_ref[0:48, :]
    for member in range(TEAM):
        out_ref[member, 0:16, :] = turned[member * SUB : (member + 1) * SUB, :]
        out_ref[member, 16:64, :] = meta


def leaf_kernel(place_ref, recv_ref, inv_hbm, out_ref, inv_ref, sem):
    inv_in = fetch(inv_hbm, inv_ref, sem)
    leaf = inv_ref.shape[0]
    slots = place_ref.shape[1]
    spread = hot(row_ids(leaf, slots) == place_ref[...])
    owned = dot(spread, recv_ref[...]).T.astype(BF)
    inv_in.wait()
    inv = inv_ref[...]
    y_t = dot(owned, inv, NT).astype(BF)
    out_ref[...] = dot(y_t, inv).T


def turn(value, shift):
    shift = shift % 128
    return pltpu.roll(value, shift, 1) if shift else value


def tree_kernel(got_ref, bare_hbm, out_ref, e0_ref, e1_ref, e2_ref, a01_ref, a02_ref, a12_ref, spots_ref):
    lane = lane_ids(32, 128)
    none = jnp.zeros((32, 128), BF)
    for peer in range(TREE):
        rows = slice(peer * 32, (peer + 1) * 32)
        low0 = jnp.zeros((32, 128), F32)
        low1 = jnp.zeros((32, 128), F32)
        for front in range(2):
            src = peer * 2 + front
            e2_ref[rows, front * 128 : (front + 1) * 128] = got_ref[src, 16:48, 0:128]
            rest = got_ref[src, 16:48, 128:256].astype(F32)
            one = jnp.where(lane < 64, rest, 0.0)
            zero = jnp.where((lane >= 64) & (lane < 96), rest, 0.0)
            low1 = low1 + turn(one, front * 64)
            low0 = low0 + turn(zero, ((peer // 2) % 2) * 64 + front * 32 - 64)
        tile = peer // 4
        for ref, low in ((e1_ref, low1), (e0_ref, low0)):
            ref[rows, tile * 128 : (tile + 1) * 128] = low.astype(BF)
            ref[rows, (1 - tile) * 128 : (2 - tile) * 128] = none
    sub = row_ids(256, 64)
    for src in range(TEAM):
        for pair, ref in enumerate((a01_ref, a02_ref, a12_ref)):
            where = got_ref[src, 48 + pair : 49 + pair, 192:256].astype(F32).astype(jnp.int32)
            if pair == 0:
                where = where + src // 8 * 128
            flipped = got_ref[src, 48:64, pair * 64 : (pair + 1) * 64]
            ref[src * SUB : (src + 1) * SUB, :] = dot(flipped, hot(sub == where), NT).astype(BF)
    wide = row_ids(256, 256)
    for level in range(3):
        for quad in range(4):
            parts = []
            for src in range(quad * 4, quad * 4 + 4):
                where = got_ref[src, 51 + level : 52 + level, 192:256].astype(F32)
                parts.append(where + (src // 4 * 64, src // 8 * 128, 0)[level])
            where = jnp.concatenate(parts, axis=1).astype(jnp.int32)
            spots_ref[level * 4 + quad] = hot(wide == where)
    lane = lane_ids(SUB, 128)
    first = lane < 64
    sums = []
    for level in range(3):
        tiles = []
        for tile in range(2):
            total = jnp.zeros((SUB, 128), F32)
            for at in range(8):
                piece = got_ref[tile * 8 + at, 0:16, 128:256].astype(F32)
                begin = 64 + level * SUB
                piece = jnp.where((lane >= begin) & (lane < begin + SUB), piece, 0.0)
                total = total + turn(piece, at * SUB - begin)
            tiles.append(total)
        rest = jnp.concatenate(tiles, axis=1)
        tile = slice(level // 2 * 128, level // 2 * 128 + 128)
        for quad in range(4):
            halves = []
            for pair in range(2):
                left = got_ref[quad * 4 + pair * 2, 0:16, tile].astype(F32)
                right = got_ref[quad * 4 + pair * 2 + 1, 0:16, tile].astype(F32)
                if level == 1:
                    halves.append(jnp.where(first, turn(left, 64), right))
                else:
                    halves.append(jnp.where(first, left, turn(right, 64)))
            moved = jnp.concatenate(halves, axis=1).astype(BF)
            rest = rest - dot(moved, spots_ref[level * 4 + quad], NT)
        sums.append(rest)
    r0, r1, r2 = sums
    e0, e1, e2 = e0_ref[...], e1_ref[...], e2_ref[...]
    a01, a02, a12 = a01_ref[...], a02_ref[...], a12_ref[...]
    y0 = dot(r0.astype(BF), e0, NT)
    y0b = y0.astype(BF)
    y1 = dot((r1 - dot(y0b, a01)).astype(BF), e1, NT)
    y1b = y1.astype(BF)
    y2 = dot((r2 - dot(y0b, a02) - dot(y1b, a12)).astype(BF), e2, NT)
    x2 = dot(y2.astype(BF), e2).astype(BF)
    x1 = dot((y1 - dot(x2, a12, NT)).astype(BF), e1).astype(BF)
    x0 = dot((y0 - dot(x2, a02, NT) - dot(x1, a01, NT)).astype(BF), e0).astype(BF)
    solved = (x0, x1, x2)
    for quad in range(4):
        picks = [dot(solved[level], spots_ref[level * 4 + quad]) for level in range(3)]
        for at in range(4):
            dst = quad * 4 + at
            half = slice(at // 2 * 128, at // 2 * 128 + 128)
            p0, p1, p2 = [pick[:, half] for pick in picks]
            if at % 2:
                p0, p2 = turn(p0, 64), turn(p2, 64)
            else:
                p1 = turn(p1, 64)
            out_ref[dst, :, 0:128] = jnp.where(first, p0, p1).astype(BF)
            rest = jnp.where(first, p2, 0.0)
            tile = slice(dst // 8 * 128, dst // 8 * 128 + 128)
            for level in range(3):
                begin = 64 + level * SUB
                piece = turn(solved[level][:, tile].astype(F32), begin - dst % 8 * SUB)
                rest = jnp.where((lane >= begin) & (lane < begin + SUB), piece, rest)
            out_ref[dst, :, 128:256] = rest.astype(BF)


def finish_kernel(got_ref, back_ref, leaf_ref, out_ref, sep_ref):
    table = got_ref[...].reshape(256, 256)
    out_ref[...] = leaf_ref[...] - dot(back_ref[...], table, NT)
    pick = hot(lane_ids(48, 256) == row_ids(48, 256) + 192)
    rows = dot(pick, table, NT).astype(BF)
    for level in range(3):
        sep_ref[level] = rows[level * SUB : (level + 1) * SUB, :]


def on_device(
    rhs_parts,
    send_order,
    recv_place,
    sep_rhs,
    leaf_inv,
    leaf_panels,
    leaf_rows,
    sep_inv,
    sep_panels,
    sep_rows,
):
    owners = lax.axis_size("tree") * lax.axis_size("peer")
    rhs = rhs_parts[0, 0]
    leaf, width = rhs.shape
    inv = leaf_inv[0, 0]
    panels = leaf_panels[0, 0].reshape(-1, leaf)
    keep = leaf // owners
    pad = -(-keep // 8) * 8
    slots = owners * pad
    sds = jax.ShapeDtypeStruct

    (sent,) = call(
        lambda *refs: send_kernel(keep, pad, *refs),
        "send_rows",
        [HB, HB],
        [(sds((slots, width), BF), HB)],
        [
            pltpu.VMEM((1, leaf), jnp.int32),
            pltpu.VMEM((leaf, width), BF),
            pltpu.VMEM((-(-(leaf - keep + pad) // 8) * 8 + 8, width), F32),
            pltpu.VMEM((slots, width), BF),
            DMA((5,)),
        ],
        flops=2 * leaf * leaf * width,
        nbytes=2 * leaf * width * 2,
        vmem=VMEM_ALL,
    )(send_order[0], rhs)
    recv = lax.all_to_all(
        sent.reshape(owners, pad, width), ("tree", "peer"), split_axis=0, concat_axis=0, tiled=True
    ).reshape(slots, width)

    place = jnp.pad(
        recv_place[0, 0].reshape(owners, keep), ((0, 0), (0, pad - keep)), constant_values=-1
    ).reshape(1, slots)
    span = jnp.swapaxes(sep_panels[0, 0], 1, 2)
    push, back, side = call(
        factor_kernel,
        "factor_products",
        [VM, VM, VM, HB, HB, HB, HB, HB],
        [(sds((192, slots), BF), VM), (sds((leaf, 256), BF), VM), (sds((112, 256), BF), VM)],
        [
            pltpu.VMEM(panels.shape, BF),
            pltpu.VMEM((leaf, leaf), BF),
            pltpu.VMEM(sep_inv.shape[2:], BF),
            pltpu.VMEM(span.shape, BF),
            pltpu.VMEM(sep_rhs.shape[2:], BF),
            DMA((5,)),
        ],
        flops=2 * 192 * leaf * (leaf + slots),
        nbytes=2 * leaf * leaf + 2 * 192 * slots + 2 * 256 * leaf,
    )(
        place,
        leaf_rows[0, 0][:, None, :],
        sep_rows[0, 0][:, None, :],
        panels,
        inv,
        sep_inv[0, 0],
        span,
        sep_rhs[0, 0],
    )
    team = ("peer", "front")
    (chunks,) = call(
        push_kernel,
        "push_updates",
        [VM, VM, VM],
        [(sds((TEAM, 64, 256), BF), VM)],
        flops=2 * 192 * slots * width,
        nbytes=2 * slots * (192 + width) + TEAM * 64 * 512,
    )(recv, push, side)
    got = lax.all_to_all(chunks, team, split_axis=0, concat_axis=0, tiled=True)

    (bare,) = call(
        leaf_kernel,
        "leaf_solve",
        [VM, VM, HB],
        [(sds((leaf, width), F32), VM)],
        [pltpu.VMEM((leaf, leaf), BF), DMA],
        flops=2 * leaf * width * (2 * leaf + slots),
        nbytes=2 * leaf * leaf + 6 * slots * width,
    )(place, recv, inv)

    square = pltpu.VMEM((256, 256), BF)
    (solved,) = call(
        tree_kernel,
        "separator_tree",
        [VM, pl.BlockSpec(memory_space=pl.ANY)],
        [(sds((TEAM, SUB, 256), BF), VM)],
        [square] * 6 + [pltpu.VMEM((12, 256, 256), BF)],
        flops=2 * 16 * 256 * 256 * 36 + 2 * 48 * 16 * 64 * 256,
        nbytes=TEAM * 80 * 512,
    )(got, bare)
    back_got = lax.all_to_all(solved, team, split_axis=0, concat_axis=0, tiled=True)

    leaf_solution, sep_solution = call(
        finish_kernel,
        "finish",
        [VM, VM, VM],
        [(sds((leaf, width), F32), VM), (sds((3, SUB, width), BF), VM)],
        flops=2 * leaf * 256 * width,
        nbytes=leaf * width * 8 + leaf * 512 + TEAM * SUB * 512,
    )(back_got, back, bare)
    return leaf_solution[None, None], sep_solution[None, None]


def solution(mesh):
    leaves, fronts = mesh.shape["leaf"], mesh.shape["front"]
    grid = Mesh(
        np.asarray(mesh.devices).reshape(leaves // TREE, TREE, fronts), ("tree", "peer", "front")
    )
    leaf = ("tree", "peer")
    in_specs = (
        P(leaf, "front", None, None),
        P(leaf, "front", None),
        P(leaf, "front", None),
        P(leaf, "front", None, None, None),
        P(leaf, "front", None, None),
        P(leaf, "front", None, None, None),
        P(leaf, "front", None, None),
        P(leaf, "front", None, None),
        P(leaf, "front", None, None, None),
        P(leaf, "front", None, None),
    )
    out_specs = (P(leaf, "front", None, None), P(leaf, "front", None, None, None))
    return jax.shard_map(
        on_device, mesh=grid, in_specs=in_specs, out_specs=out_specs, check_vma=False
    )
```

```python
import jax
import jax.numpy as jnp
import numpy as np
from jax import lax
from jax.experimental import pallas as pl
from jax.experimental.pallas import tpu as pltpu
from jax.sharding import Mesh, PartitionSpec as P

BF = jnp.bfloat16
F32 = jnp.float32
SUB = 16
TREE = 8
COLS = 32
VMEM_CAP = 40 * 1024 * 1024
VMEM_ALL = 62 * 1024 * 1024

NN = (((1,), (0,)), ((), ()))
NT = (((1,), (1,)), ((), ()))


def dot(a, b, dims=NN):
    return lax.dot_general(a, b, dims, preferred_element_type=F32)


def lane_ids(rows, cols):
    return lax.broadcasted_iota(jnp.int32, (rows, cols), 1)


def row_ids(rows, cols):
    return lax.broadcasted_iota(jnp.int32, (rows, cols), 0)


def hot(mask):
    return jnp.where(mask, 1.0, 0.0).astype(BF)


VM = pl.BlockSpec(memory_space=pltpu.VMEM)
SM = pl.BlockSpec(memory_space=pltpu.SMEM)
HB = pl.BlockSpec(memory_space=pltpu.HBM)
DMA = pltpu.SemaphoreType.DMA


def call(kernel, name, ins, outs, scratch=(), flops=0, nbytes=0, vmem=VMEM_CAP):
    return pl.pallas_call(
        kernel,
        out_shape=[shape for shape, _ in outs],
        in_specs=list(ins),
        out_specs=[spec for _, spec in outs],
        scratch_shapes=list(scratch),
        compiler_params=pltpu.CompilerParams(vmem_limit_bytes=vmem),
        cost_estimate=pl.CostEstimate(flops=flops, bytes_accessed=nbytes, transcendentals=0),
        name=name,
    )


def fetch(source, target, sem):
    copy = pltpu.make_async_copy(source, target, sem)
    copy.start()
    return copy


def send_kernel(keep, pad, order_hbm, rhs_hbm, out_hbm, order_ref, rhs_ref, picked_ref, out_ref, sems):
    rows, width = rhs_ref.shape
    order_in = fetch(order_hbm, order_ref, sems.at[0])
    rhs_in = fetch(rhs_hbm, rhs_ref, sems.at[1])
    tail = picked_ref.shape[0] - rows
    picked_ref[rows:, :] = jnp.zeros((tail, width), F32)
    owners = rows // keep
    step = 384
    lanes = lane_ids(128, rows)
    order_in.wait()
    hots = []
    for at in range(0, rows, 128):
        ids = jnp.broadcast_to(order_ref[:, at : at + 128], (128, 128)).T
        hots.append(hot(jnp.concatenate([ids] * (rows // 128), axis=1) == lanes))
    rhs_in.wait()
    rhs = rhs_ref[...]
    done = 0
    leaving = []
    for part in range(rows // step):
        block = jnp.concatenate(hots[part * 3 : part * 3 + 3], axis=0)
        picked_ref[part * step : (part + 1) * step, :] = dot(block, rhs)
        have = (part + 1) * step
        upto = owners if have == rows else ((have - pad) // keep + 1) // 2 * 2
        for owner in range(done, upto):
            out_ref[owner * pad : (owner + 1) * pad, :] = picked_ref[
                owner * keep : owner * keep + pad, :
            ].astype(BF)
        span = slice(done * pad, upto * pad)
        leaving.append(fetch(out_ref.at[span, :], out_hbm.at[span, :], sems.at[2 + part]))
        done = upto
    for copy in leaving:
        copy.wait()


def factor_kernel(
    place_ref, rows_ref, srow_ref, panels_hbm, inv_hbm, sinv_hbm, span_hbm, srhs_hbm,
    push_ref, back_ref, side_ref, panels_ref, inv_ref, sinv_ref, span_ref, srhs_ref, sems,
):
    moves = [
        fetch(sinv_hbm, sinv_ref, sems.at[0]),
        fetch(span_hbm, span_ref, sems.at[1]),
        fetch(srhs_hbm, srhs_ref, sems.at[2]),
        fetch(panels_hbm, panels_ref, sems.at[3]),
        fetch(inv_hbm, inv_ref, sems.at[4]),
    ]
    leaf = inv_ref.shape[0]
    slots = place_ref.shape[1]
    upd = rows_ref.shape[2]
    spread = hot(row_ids(leaf, slots) == place_ref[...])
    for move in moves:
        move.wait()
    cuts = [(low, min(low + 256, leaf)) for low in range(0, leaf, 256)]
    product = [dot(panels_ref[:, low:], inv_ref[low:, low:high]) for low, high in cuts]
    product = jnp.concatenate(product, axis=1)
    push_ref[...] = dot(product.astype(BF), spread).astype(BF)
    padded = jnp.concatenate([product, jnp.zeros((256 - product.shape[0], leaf), F32)], axis=0)
    back_ref[...] = padded.T.astype(BF)
    cols = sinv_ref.shape[1]
    lane = lane_ids(cols, 256)
    source = jnp.where(
        lane < 128, lane + 96, jnp.where(lane < 192, lane - 96, jnp.where(lane < 224, lane - 192, -1))
    )
    side_ref[0:32, :] = dot(sinv_ref[...], hot(row_ids(cols, 256) == source)).astype(BF)
    lists = [srow_ref[pair].astype(F32) for pair in range(3)]
    lists += [rows_ref[level].astype(F32) for level in range(3)]
    lists = jnp.concatenate(lists + [jnp.zeros((SUB - 6, upd), F32)], axis=0)
    flipped = [span_ref[pair].astype(F32) for pair in range(3)]
    side_ref[32:48, :] = jnp.concatenate(flipped + [lists], axis=1).astype(BF)
    for level in range(3):
        side_ref[48 + level * SUB : 64 + level * SUB, :] = srhs_ref[level]
    side_ref[96:112, :] = jnp.zeros((SUB, 256), BF)


def push_kernel(recv_ref, push_ref, side_ref, out_ref):
    sums = dot(push_ref[...], recv_ref[...])
    rows = jnp.concatenate([sums, side_ref[48:112, :].astype(F32)], axis=0)
    turned = rows.T.astype(BF)
    meta = side_ref[0:48, :]
    for peer in range(TREE):
        out_ref[peer, 0:32, :] = turned[peer * COLS : (peer + 1) * COLS, :]
        out_ref[peer, 32:80, :] = meta


def leaf_kernel(place_ref, recv_ref, inv_hbm, out_ref, inv_ref, sem):
    inv_in = fetch(inv_hbm, inv_ref, sem)
    leaf = inv_ref.shape[0]
    slots = place_ref.shape[1]
    spread = hot(row_ids(leaf, slots) == place_ref[...])
    owned = dot(spread, recv_ref[...]).T.astype(BF)
    inv_in.wait()
    cuts = [(low, min(low + 256, leaf)) for low in range(0, leaf, 256)]
    y_t = [dot(owned[:, :high], inv_ref[low:high, :high], NT) for low, high in cuts]
    y_t = jnp.concatenate(y_t, axis=1).astype(BF)
    bare_t = [dot(y_t[:, low:], inv_ref[low:, low:high]) for low, high in cuts]
    out_ref[...] = jnp.concatenate(bare_t, axis=1).T


def turn(value, shift):
    shift = shift % 128
    return pltpu.roll(value, shift, 1) if shift else value


def tree_kernel(
    front_ref, got_ref, other_ref, bare_hbm, out_ref,
    e0_ref, e1_ref, e2_ref, a01_ref, a02_ref, a12_ref, spots_ref,
):
    front = front_ref[0]
    first = front == 0
    sides = (got_ref, other_ref)
    lane = lane_ids(32, 128)
    none = jnp.zeros((32, 128), BF)
    for peer in range(TREE):
        rows = slice(peer * 32, (peer + 1) * 32)
        mine = got_ref[peer, 32:64, :].astype(F32)
        theirs = other_ref[peer, 32:64, :].astype(F32)
        left = jnp.where(first, mine, theirs)
        right = jnp.where(first, theirs, mine)
        e2_ref[rows, 0:128] = left[:, 0:128].astype(BF)
        e2_ref[rows, 128:256] = right[:, 0:128].astype(BF)
        left, right = left[:, 128:256], right[:, 128:256]
        low1 = jnp.where(lane < 64, left, turn(right, 64))
        inside = (lane >= 64) & (lane < 96)
        to = ((peer // 2) % 2) * 64
        low0 = turn(jnp.where(inside, left, 0.0), to - 64)
        low0 = low0 + turn(jnp.where(inside, right, 0.0), to + 32 - 64)
        tile = peer // 4
        for ref, low in ((e1_ref, low1), (e0_ref, low0)):
            ref[rows, tile * 128 : (tile + 1) * 128] = low.astype(BF)
            ref[rows, (1 - tile) * 128 : (2 - tile) * 128] = none
    sub = row_ids(256, 64)
    for side, table in enumerate(sides):
        for peer in range(TREE):
            at = peer * 2 * SUB + (front ^ side) * SUB
            rows = pl.ds(pl.multiple_of(at, SUB), SUB)
            for pair, ref in enumerate((a01_ref, a02_ref, a12_ref)):
                where = table[peer, 64 + pair : 65 + pair, 192:256].astype(F32).astype(jnp.int32)
                if pair == 0:
                    where = where + peer // 4 * 128
                flipped = table[peer, 64:80, pair * 64 : (pair + 1) * 64]
                ref[rows, :] = dot(flipped, hot(sub == where), NT).astype(BF)
    wide = row_ids(256, 256)
    for level in range(3):
        for quad in range(4):
            parts = []
            for peer in range(quad % 2 * 4, quad % 2 * 4 + 4):
                where = sides[quad // 2][peer, 67 + level : 68 + level, 192:256].astype(F32)
                parts.append(where + (peer // 2 * 64, peer // 4 * 128, 0)[level])
            where = jnp.concatenate(parts, axis=1).astype(jnp.int32)
            spots_ref[level * 4 + quad] = hot(wide == where)
    lane = lane_ids(COLS, 128)
    half = lane < 64
    sums = []
    for level in range(3):
        begin = 64 + level * SUB
        inside = (lane >= begin) & (lane < begin + SUB)
        tiles = []
        for tile in range(2):
            totals = []
            for table in sides:
                total = jnp.zeros((COLS, 128), F32)
                for at in range(4):
                    piece = table[tile * 4 + at, 0:32, 128:256].astype(F32)
                    total = total + turn(jnp.where(inside, piece, 0.0), at * 32 - begin)
                totals.append(total)
            mine, theirs = totals
            left = jnp.where(first, mine, theirs)
            right = jnp.where(first, theirs, mine)
            tiles.append(left + turn(right, SUB))
        rest = jnp.concatenate(tiles, axis=1)
        tile = slice(level // 2 * 128, level // 2 * 128 + 128)
        for quad in range(4):
            table = sides[quad // 2]
            halves = []
            for pair in range(2):
                peer = quad % 2 * 4 + pair * 2
                left = table[peer, 0:32, tile].astype(F32)
                right = table[peer + 1, 0:32, tile].astype(F32)
                if level == 1:
                    halves.append(jnp.where(half, turn(left, 64), right))
                else:
                    halves.append(jnp.where(half, left, turn(right, 64)))
            moved = jnp.concatenate(halves, axis=1).astype(BF)
            rest = rest - dot(moved, spots_ref[level * 4 + quad], NT)
        sums.append(rest)
    r0, r1, r2 = sums
    e0, e1, e2 = e0_ref[...], e1_ref[...], e2_ref[...]
    a01, a02, a12 = a01_ref[...], a02_ref[...], a12_ref[...]
    y0 = dot(r0.astype(BF), e0, NT)
    y0b = y0.astype(BF)
    y1 = dot((r1 - dot(y0b, a01)).astype(BF), e1, NT)
    y1b = y1.astype(BF)
    y2 = dot((r2 - dot(y0b, a02) - dot(y1b, a12)).astype(BF), e2, NT)
    x2 = dot(y2.astype(BF), e2).astype(BF)
    x1 = dot((y1 - dot(x2, a12, NT)).astype(BF), e1).astype(BF)
    x0 = dot((y0 - dot(x2, a02, NT) - dot(x1, a01, NT)).astype(BF), e0).astype(BF)
    solved = (x0, x1, x2)
    own = []
    for level in range(3):
        for tile in range(2):
            piece = solved[level][:, tile * 128 : (tile + 1) * 128].astype(F32)
            own.append(jnp.where(first, piece, turn(piece, -SUB)))
    for quad in range(2):
        picks = [dot(solved[level], spots_ref[level * 4 + quad]) for level in range(3)]
        for at in range(4):
            peer = quad * 4 + at
            part = slice(at // 2 * 128, at // 2 * 128 + 128)
            p0, p1, p2 = [pick[:, part] for pick in picks]
            if at % 2:
                p0, p2 = turn(p0, 64), turn(p2, 64)
            else:
                p1 = turn(p1, 64)
            out_ref[peer, :, 0:128] = jnp.where(half, p0, p1).astype(BF)
            rest = jnp.where(half, p2, 0.0)
            for level in range(3):
                begin = 64 + level * SUB
                piece = turn(own[level * 2 + quad], begin - at * 32)
                rest = jnp.where((lane >= begin) & (lane < begin + SUB), piece, rest)
            out_ref[peer, :, 128:256] = rest.astype(BF)


def finish_kernel(got_ref, back_ref, leaf_ref, out_ref, sep_ref):
    table = got_ref[...].reshape(256, 256)
    out_ref[...] = leaf_ref[...] - dot(back_ref[...], table, NT)
    pick = hot(lane_ids(48, 256) == row_ids(48, 256) + 192)
    rows = dot(pick, table, NT).astype(BF)
    for level in range(3):
        sep_ref[level] = rows[level * SUB : (level + 1) * SUB, :]


def on_device(
    rhs_parts,
    send_order,
    recv_place,
    sep_rhs,
    leaf_inv,
    leaf_panels,
    leaf_rows,
    sep_inv,
    sep_panels,
    sep_rows,
):
    owners = lax.axis_size("tree") * lax.axis_size("peer")
    rhs = rhs_parts[0, 0]
    leaf, width = rhs.shape
    inv = leaf_inv[0, 0]
    panels = leaf_panels[0, 0].reshape(-1, leaf)
    keep = leaf // owners
    pad = -(-keep // 8) * 8
    slots = owners * pad
    sds = jax.ShapeDtypeStruct

    (sent,) = call(
        lambda *refs: send_kernel(keep, pad, *refs),
        "send_rows",
        [HB, HB],
        [(sds((slots, width), BF), HB)],
        [
            pltpu.VMEM((1, leaf), jnp.int32),
            pltpu.VMEM((leaf, width), BF),
            pltpu.VMEM((-(-(leaf - keep + pad) // 8) * 8 + 8, width), F32),
            pltpu.VMEM((slots, width), BF),
            DMA((5,)),
        ],
        flops=2 * leaf * leaf * width,
        nbytes=2 * leaf * width * 2,
        vmem=VMEM_ALL,
    )(send_order[0], rhs)
    recv = lax.all_to_all(
        sent.reshape(owners, pad, width), ("tree", "peer"), split_axis=0, concat_axis=0, tiled=True
    ).reshape(slots, width)

    place = jnp.pad(
        recv_place[0, 0].reshape(owners, keep), ((0, 0), (0, pad - keep)), constant_values=-1
    ).reshape(1, slots)
    span = jnp.swapaxes(sep_panels[0, 0], 1, 2)
    push, back, side = call(
        factor_kernel,
        "factor_products",
        [VM, VM, VM, HB, HB, HB, HB, HB],
        [(sds((192, slots), BF), VM), (sds((leaf, 256), BF), VM), (sds((112, 256), BF), VM)],
        [
            pltpu.VMEM(panels.shape, BF),
            pltpu.VMEM((leaf, leaf), BF),
            pltpu.VMEM(sep_inv.shape[2:], BF),
            pltpu.VMEM(span.shape, BF),
            pltpu.VMEM(sep_rhs.shape[2:], BF),
            DMA((5,)),
        ],
        flops=2 * 192 * leaf * (leaf + slots),
        nbytes=2 * leaf * leaf + 2 * 192 * slots + 2 * 256 * leaf,
    )(
        place,
        leaf_rows[0, 0][:, None, :],
        sep_rows[0, 0][:, None, :],
        panels,
        inv,
        sep_inv[0, 0],
        span,
        sep_rhs[0, 0],
    )
    (chunks,) = call(
        push_kernel,
        "push_updates",
        [VM, VM, VM],
        [(sds((TREE, 80, 256), BF), VM)],
        flops=2 * 192 * slots * width,
        nbytes=2 * slots * (192 + width) + TREE * 80 * 512,
    )(recv, push, side)
    got = lax.all_to_all(chunks, "peer", split_axis=0, concat_axis=0, tiled=True)
    (bare,) = call(
        leaf_kernel,
        "leaf_solve",
        [VM, VM, HB],
        [(sds((leaf, width), F32), VM)],
        [pltpu.VMEM((leaf, leaf), BF), DMA],
        flops=2 * leaf * width * (2 * leaf + slots),
        nbytes=2 * leaf * leaf + 6 * slots * width,
    )(place, recv, inv)

    got, bare = lax.optimization_barrier((got, bare))
    other = lax.ppermute(got, "front", [(0, 1), (1, 0)])
    front = lax.axis_index("front").astype(jnp.int32).reshape(1)
    square = pltpu.VMEM((256, 256), BF)
    (solved,) = call(
        tree_kernel,
        "separator_tree",
        [SM, VM, VM, pl.BlockSpec(memory_space=pl.ANY)],
        [(sds((TREE, COLS, 256), BF), VM)],
        [square] * 6 + [pltpu.VMEM((12, 256, 256), BF)],
        flops=2 * 32 * 256 * 256 * 30 + 2 * 48 * 16 * 64 * 256,
        nbytes=TREE * 192 * 512,
    )(front, got, other, bare)
    back_got = lax.all_to_all(solved, "peer", split_axis=0, concat_axis=0, tiled=True)

    leaf_solution, sep_solution = call(
        finish_kernel,
        "finish",
        [VM, VM, VM],
        [(sds((leaf, width), F32), VM), (sds((3, SUB, width), BF), VM)],
        flops=2 * leaf * 256 * width,
        nbytes=leaf * width * 8 + leaf * 512 + TREE * COLS * 512,
    )(back_got, back, bare)
    return leaf_solution[None, None], sep_solution[None, None]


def solution(mesh):
    leaves, fronts = mesh.shape["leaf"], mesh.shape["front"]
    grid = Mesh(
        np.asarray(mesh.devices).reshape(leaves // TREE, TREE, fronts), ("tree", "peer", "front")
    )
    leaf = ("tree", "peer")
    in_specs = (
        P(leaf, "front", None, None),
        P(leaf, "front", None),
        P(leaf, "front", None),
        P(leaf, "front", None, None, None),
        P(leaf, "front", None, None),
        P(leaf, "front", None, None, None),
        P(leaf, "front", None, None),
        P(leaf, "front", None, None),
        P(leaf, "front", None, None, None),
        P(leaf, "front", None, None),
    )
    out_specs = (P(leaf, "front", None, None), P(leaf, "front", None, None, None))
    return jax.shard_map(
        on_device, mesh=grid, in_specs=in_specs, out_specs=out_specs, check_vma=False
    )
```

```python
import jax
import jax.numpy as jnp
import numpy as np
from jax import lax
from jax.experimental import pallas as pl
from jax.experimental.pallas import tpu as pltpu
from jax.sharding import Mesh, PartitionSpec as P

BF = jnp.bfloat16
F32 = jnp.float32
SUB = 16
TREE = 8
COLS = 32
VMEM_CAP = 40 * 1024 * 1024
VMEM_ALL = 62 * 1024 * 1024

NN = (((1,), (0,)), ((), ()))
NT = (((1,), (1,)), ((), ()))


def dot(a, b, dims=NN):
    return lax.dot_general(a, b, dims, preferred_element_type=F32)


def lane_ids(rows, cols):
    return lax.broadcasted_iota(jnp.int32, (rows, cols), 1)


def row_ids(rows, cols):
    return lax.broadcasted_iota(jnp.int32, (rows, cols), 0)


def hot(mask):
    return jnp.where(mask, 1.0, 0.0).astype(BF)


VM = pl.BlockSpec(memory_space=pltpu.VMEM)
SM = pl.BlockSpec(memory_space=pltpu.SMEM)
HB = pl.BlockSpec(memory_space=pltpu.HBM)
DMA = pltpu.SemaphoreType.DMA


def call(kernel, name, ins, outs, scratch=(), flops=0, nbytes=0, vmem=VMEM_CAP):
    return pl.pallas_call(
        kernel,
        out_shape=[shape for shape, _ in outs],
        in_specs=list(ins),
        out_specs=[spec for _, spec in outs],
        scratch_shapes=list(scratch),
        compiler_params=pltpu.CompilerParams(vmem_limit_bytes=vmem),
        cost_estimate=pl.CostEstimate(flops=flops, bytes_accessed=nbytes, transcendentals=0),
        name=name,
    )


def fetch(source, target, sem):
    copy = pltpu.make_async_copy(source, target, sem)
    copy.start()
    return copy


def send_kernel(keep, pad, order_hbm, rhs_hbm, out_hbm, order_ref, rhs_ref, picked_ref, out_ref, sems):
    rows, width = rhs_ref.shape
    order_in = fetch(order_hbm, order_ref, sems.at[0])
    rhs_in = fetch(rhs_hbm, rhs_ref, sems.at[1])
    tail = picked_ref.shape[0] - rows
    picked_ref[rows:, :] = jnp.zeros((tail, width), F32)
    owners = rows // keep
    step = 384
    lanes = lane_ids(128, rows)
    order_in.wait()
    hots = []
    for at in range(0, rows, 128):
        ids = jnp.broadcast_to(order_ref[:, at : at + 128], (128, 128)).T
        hots.append(hot(jnp.concatenate([ids] * (rows // 128), axis=1) == lanes))
    rhs_in.wait()
    rhs = rhs_ref[...]
    done = 0
    leaving = []
    for part in range(rows // step):
        block = jnp.concatenate(hots[part * 3 : part * 3 + 3], axis=0)
        picked_ref[part * step : (part + 1) * step, :] = dot(block, rhs)
        have = (part + 1) * step
        upto = owners if have == rows else ((have - pad) // keep + 1) // 2 * 2
        for owner in range(done, upto):
            out_ref[owner * pad : (owner + 1) * pad, :] = picked_ref[
                owner * keep : owner * keep + pad, :
            ].astype(BF)
        span = slice(done * pad, upto * pad)
        leaving.append(fetch(out_ref.at[span, :], out_hbm.at[span, :], sems.at[2 + part]))
        done = upto
    for copy in leaving:
        copy.wait()


def column_cuts(leaf):
    cuts, base = [], 0
    for low in range(0, leaf, 256):
        cuts.append((low, min(low + 256, leaf), base))
        base += leaf - low
    return cuts


def factor_kernel(
    place_ref, rows_ref, srow_ref, inv_ref, panels_hbm, sinv_hbm, span_hbm, srhs_hbm,
    push_ref, back_ref, side_ref, packed_hbm, panels_ref, sinv_ref, span_ref, srhs_ref, sems,
):
    moves = [
        fetch(sinv_hbm, sinv_ref, sems.at[0]),
        fetch(span_hbm, span_ref, sems.at[1]),
        fetch(srhs_hbm, srhs_ref, sems.at[2]),
        fetch(panels_hbm, panels_ref, sems.at[3]),
    ]
    leaf = inv_ref.shape[0]
    slots = place_ref.shape[1]
    upd = rows_ref.shape[2]
    cuts = column_cuts(leaf)
    leaving = [
        fetch(
            inv_ref.at[low:leaf, low:high],
            packed_hbm.at[base : base + leaf - low, 0 : high - low],
            sems.at[4 + at],
        )
        for at, (low, high, base) in enumerate(cuts)
    ]
    spread = hot(row_ids(leaf, slots) == place_ref[...])
    for move in moves:
        move.wait()
    product = [dot(panels_ref[:, low:], inv_ref[low:, low:high]) for low, high, _ in cuts]
    product = jnp.concatenate(product, axis=1)
    push_ref[...] = dot(product.astype(BF), spread).astype(BF)
    padded = jnp.concatenate([product, jnp.zeros((256 - product.shape[0], leaf), F32)], axis=0)
    back_ref[...] = padded.T.astype(BF)
    cols = sinv_ref.shape[1]
    lane = lane_ids(cols, 256)
    source = jnp.where(
        lane < 128, lane + 96, jnp.where(lane < 192, lane - 96, jnp.where(lane < 224, lane - 192, -1))
    )
    side_ref[0:32, :] = dot(sinv_ref[...], hot(row_ids(cols, 256) == source)).astype(BF)
    lists = [srow_ref[pair].astype(F32) for pair in range(3)]
    lists += [rows_ref[level].astype(F32) for level in range(3)]
    lists = jnp.concatenate(lists + [jnp.zeros((SUB - 6, upd), F32)], axis=0)
    flipped = [span_ref[pair].astype(F32) for pair in range(3)]
    side_ref[32:48, :] = jnp.concatenate(flipped + [lists], axis=1).astype(BF)
    for level in range(3):
        side_ref[48 + level * SUB : 64 + level * SUB, :] = srhs_ref[level]
    side_ref[96:112, :] = jnp.zeros((SUB, 256), BF)
    for copy in leaving:
        copy.wait()


def push_kernel(recv_ref, push_ref, side_ref, out_ref):
    sums = dot(push_ref[...], recv_ref[...])
    rows = jnp.concatenate([sums, side_ref[48:112, :].astype(F32)], axis=0)
    turned = rows.T.astype(BF)
    meta = side_ref[0:48, :]
    for peer in range(TREE):
        out_ref[peer, 0:32, :] = turned[peer * COLS : (peer + 1) * COLS, :]
        out_ref[peer, 32:80, :] = meta


def forward_kernel(leaf, place_ref, recv_ref, packed_ref, y_ref):
    slots = place_ref.shape[1]
    spread = hot(row_ids(leaf, slots) == place_ref[...])
    owned = dot(spread, recv_ref[...]).T.astype(BF)
    cuts = column_cuts(leaf)
    y_t = []
    for low, high, _ in cuts:
        total = None
        for left, right, base in cuts:
            if left <= low:
                rows = slice(base + low - left, base + high - left)
                term = dot(owned[:, left:right], packed_ref[rows, 0 : right - left], NT)
                total = term if total is None else total + term
        y_t.append(total)
    y_ref[...] = jnp.concatenate(y_t, axis=1).astype(BF)


def backward_kernel(y_ref, packed_ref, out_ref):
    leaf = out_ref.shape[0]
    cuts = column_cuts(leaf)
    y_t = y_ref[...]
    bare_t = [
        dot(y_t[:, low:], packed_ref[base : base + leaf - low, 0 : high - low])
        for low, high, base in cuts
    ]
    out_ref[...] = jnp.concatenate(bare_t, axis=1).T


def turn(value, shift):
    shift = shift % 128
    return pltpu.roll(value, shift, 1) if shift else value


def tree_kernel(
    front_ref, got_ref, other_ref, bare_hbm, out_ref,
    e0_ref, e1_ref, e2_ref, a01_ref, a02_ref, a12_ref, spots_ref,
):
    front = front_ref[0]
    first = front == 0
    sides = (got_ref, other_ref)
    lane = lane_ids(32, 128)
    none = jnp.zeros((32, 128), BF)
    for peer in range(TREE):
        rows = slice(peer * 32, (peer + 1) * 32)
        mine = got_ref[peer, 32:64, :].astype(F32)
        theirs = other_ref[peer, 32:64, :].astype(F32)
        left = jnp.where(first, mine, theirs)
        right = jnp.where(first, theirs, mine)
        e2_ref[rows, 0:128] = left[:, 0:128].astype(BF)
        e2_ref[rows, 128:256] = right[:, 0:128].astype(BF)
        left, right = left[:, 128:256], right[:, 128:256]
        low1 = jnp.where(lane < 64, left, turn(right, 64))
        inside = (lane >= 64) & (lane < 96)
        to = ((peer // 2) % 2) * 64
        low0 = turn(jnp.where(inside, left, 0.0), to - 64)
        low0 = low0 + turn(jnp.where(inside, right, 0.0), to + 32 - 64)
        tile = peer // 4
        for ref, low in ((e1_ref, low1), (e0_ref, low0)):
            ref[rows, tile * 128 : (tile + 1) * 128] = low.astype(BF)
            ref[rows, (1 - tile) * 128 : (2 - tile) * 128] = none
    sub = row_ids(256, 64)
    for side, table in enumerate(sides):
        for peer in range(TREE):
            at = peer * 2 * SUB + (front ^ side) * SUB
            rows = pl.ds(pl.multiple_of(at, SUB), SUB)
            for pair, ref in enumerate((a01_ref, a02_ref, a12_ref)):
                where = table[peer, 64 + pair : 65 + pair, 192:256].astype(F32).astype(jnp.int32)
                if pair == 0:
                    where = where + peer // 4 * 128
                flipped = table[peer, 64:80, pair * 64 : (pair + 1) * 64]
                ref[rows, :] = dot(flipped, hot(sub == where), NT).astype(BF)
    wide = row_ids(256, 256)
    for level in range(3):
        for quad in range(4):
            parts = []
            for peer in range(quad % 2 * 4, quad % 2 * 4 + 4):
                where = sides[quad // 2][peer, 67 + level : 68 + level, 192:256].astype(F32)
                parts.append(where + (peer // 2 * 64, peer // 4 * 128, 0)[level])
            where = jnp.concatenate(parts, axis=1).astype(jnp.int32)
            spots_ref[level * 4 + quad] = hot(wide == where)
    lane = lane_ids(COLS, 128)
    half = lane < 64
    sums = []
    for level in range(3):
        begin = 64 + level * SUB
        inside = (lane >= begin) & (lane < begin + SUB)
        tiles = []
        for tile in range(2):
            totals = []
            for table in sides:
                total = jnp.zeros((COLS, 128), F32)
                for at in range(4):
                    piece = table[tile * 4 + at, 0:32, 128:256].astype(F32)
                    total = total + turn(jnp.where(inside, piece, 0.0), at * 32 - begin)
                totals.append(total)
            mine, theirs = totals
            left = jnp.where(first, mine, theirs)
            right = jnp.where(first, theirs, mine)
            tiles.append(left + turn(right, SUB))
        rest = jnp.concatenate(tiles, axis=1)
        tile = slice(level // 2 * 128, level // 2 * 128 + 128)
        for quad in range(4):
            table = sides[quad // 2]
            halves = []
            for pair in range(2):
                peer = quad % 2 * 4 + pair * 2
                left = table[peer, 0:32, tile].astype(F32)
                right = table[peer + 1, 0:32, tile].astype(F32)
                if level == 1:
                    halves.append(jnp.where(half, turn(left, 64), right))
                else:
                    halves.append(jnp.where(half, left, turn(right, 64)))
            moved = jnp.concatenate(halves, axis=1).astype(BF)
            rest = rest - dot(moved, spots_ref[level * 4 + quad], NT)
        sums.append(rest)
    r0, r1, r2 = sums
    e0, e1, e2 = e0_ref[...], e1_ref[...], e2_ref[...]
    a01, a02, a12 = a01_ref[...], a02_ref[...], a12_ref[...]
    y0 = dot(r0.astype(BF), e0, NT)
    y0b = y0.astype(BF)
    y1 = dot((r1 - dot(y0b, a01)).astype(BF), e1, NT)
    y1b = y1.astype(BF)
    y2 = dot((r2 - dot(y0b, a02) - dot(y1b, a12)).astype(BF), e2, NT)
    x2 = dot(y2.astype(BF), e2).astype(BF)
    x1 = dot((y1 - dot(x2, a12, NT)).astype(BF), e1).astype(BF)
    x0 = dot((y0 - dot(x2, a02, NT) - dot(x1, a01, NT)).astype(BF), e0).astype(BF)
    solved = (x0, x1, x2)
    own = []
    for level in range(3):
        for tile in range(2):
            piece = solved[level][:, tile * 128 : (tile + 1) * 128].astype(F32)
            own.append(jnp.where(first, piece, turn(piece, -SUB)))
    for quad in range(2):
        picks = [dot(solved[level], spots_ref[level * 4 + quad]) for level in range(3)]
        for at in range(4):
            peer = quad * 4 + at
            part = slice(at // 2 * 128, at // 2 * 128 + 128)
            p0, p1, p2 = [pick[:, part] for pick in picks]
            if at % 2:
                p0, p2 = turn(p0, 64), turn(p2, 64)
            else:
                p1 = turn(p1, 64)
            out_ref[peer, :, 0:128] = jnp.where(half, p0, p1).astype(BF)
            rest = jnp.where(half, p2, 0.0)
            for level in range(3):
                begin = 64 + level * SUB
                piece = turn(own[level * 2 + quad], begin - at * 32)
                rest = jnp.where((lane >= begin) & (lane < begin + SUB), piece, rest)
            out_ref[peer, :, 128:256] = rest.astype(BF)


def finish_kernel(got_ref, back_ref, leaf_ref, out_ref, sep_ref):
    table = got_ref[...].reshape(256, 256)
    out_ref[...] = leaf_ref[...] - dot(back_ref[...], table, NT)
    pick = hot(lane_ids(48, 256) == row_ids(48, 256) + 192)
    rows = dot(pick, table, NT).astype(BF)
    for level in range(3):
        sep_ref[level] = rows[level * SUB : (level + 1) * SUB, :]


def on_device(
    rhs_parts,
    send_order,
    recv_place,
    sep_rhs,
    leaf_inv,
    leaf_panels,
    leaf_rows,
    sep_inv,
    sep_panels,
    sep_rows,
):
    owners = lax.axis_size("tree") * lax.axis_size("peer")
    rhs = rhs_parts[0, 0]
    leaf, width = rhs.shape
    inv = leaf_inv[0, 0]
    panels = leaf_panels[0, 0].reshape(-1, leaf)
    keep = leaf // owners
    pad = -(-keep // 8) * 8
    slots = owners * pad
    sds = jax.ShapeDtypeStruct

    (sent,) = call(
        lambda *refs: send_kernel(keep, pad, *refs),
        "send_rows",
        [HB, HB],
        [(sds((slots, width), BF), HB)],
        [
            pltpu.VMEM((1, leaf), jnp.int32),
            pltpu.VMEM((leaf, width), BF),
            pltpu.VMEM((-(-(leaf - keep + pad) // 8) * 8 + 8, width), F32),
            pltpu.VMEM((slots, width), BF),
            DMA((5,)),
        ],
        flops=2 * leaf * leaf * width,
        nbytes=2 * leaf * width * 2,
        vmem=VMEM_ALL,
    )(send_order[0], rhs)
    recv = lax.all_to_all(
        sent.reshape(owners, pad, width), ("tree", "peer"), split_axis=0, concat_axis=0, tiled=True
    ).reshape(slots, width)

    place = jnp.pad(
        recv_place[0, 0].reshape(owners, keep), ((0, 0), (0, pad - keep)), constant_values=-1
    ).reshape(1, slots)
    span = jnp.swapaxes(sep_panels[0, 0], 1, 2)
    packed_rows = sum(leaf - low for low, _, _ in column_cuts(leaf))
    push, back, side, packed = call(
        factor_kernel,
        "factor_products",
        [VM, VM, VM, VM, HB, HB, HB, HB],
        [
            (sds((192, slots), BF), VM),
            (sds((leaf, 256), BF), VM),
            (sds((112, 256), BF), VM),
            (sds((packed_rows, 256), BF), HB),
        ],
        [
            pltpu.VMEM(panels.shape, BF),
            pltpu.VMEM(sep_inv.shape[2:], BF),
            pltpu.VMEM(span.shape, BF),
            pltpu.VMEM(sep_rhs.shape[2:], BF),
            DMA((4 + len(column_cuts(leaf)),)),
        ],
        flops=2 * 192 * leaf * (leaf + slots),
        nbytes=2 * leaf * leaf + 2 * 192 * slots + 2 * 256 * leaf,
    )(
        place,
        leaf_rows[0, 0][:, None, :],
        sep_rows[0, 0][:, None, :],
        inv,
        panels,
        sep_inv[0, 0],
        span,
        sep_rhs[0, 0],
    )
    (chunks,) = call(
        push_kernel,
        "push_updates",
        [VM, VM, VM],
        [(sds((TREE, 80, 256), BF), VM)],
        flops=2 * 192 * slots * width,
        nbytes=2 * slots * (192 + width) + TREE * 80 * 512,
    )(recv, push, side)
    got = lax.all_to_all(chunks, "peer", split_axis=0, concat_axis=0, tiled=True)
    (leaf_y,) = call(
        lambda *refs: forward_kernel(leaf, *refs),
        "leaf_forward",
        [VM, VM, VM],
        [(sds((width, leaf), BF), VM)],
        flops=2 * leaf * width * (leaf + slots),
        nbytes=2 * leaf * leaf + 4 * slots * width,
    )(place, recv, packed)
    got, leaf_y = lax.optimization_barrier((got, leaf_y))
    other = lax.ppermute(got, "front", [(0, 1), (1, 0)])
    front = lax.axis_index("front").astype(jnp.int32).reshape(1)
    (bare,) = call(
        backward_kernel,
        "leaf_backward",
        [VM, VM],
        [(sds((leaf, width), F32), VM)],
        flops=2 * leaf * width * leaf,
        nbytes=2 * leaf * leaf + 6 * leaf * width,
    )(leaf_y, packed)
    square = pltpu.VMEM((256, 256), BF)
    (solved,) = call(
        tree_kernel,
        "separator_tree",
        [SM, VM, VM, pl.BlockSpec(memory_space=pl.ANY)],
        [(sds((TREE, COLS, 256), BF), VM)],
        [square] * 6 + [pltpu.VMEM((12, 256, 256), BF)],
        flops=2 * 32 * 256 * 256 * 30 + 2 * 48 * 16 * 64 * 256,
        nbytes=TREE * 192 * 512,
    )(front, got, other, bare)
    back_got = lax.all_to_all(solved, "peer", split_axis=0, concat_axis=0, tiled=True)

    leaf_solution, sep_solution = call(
        finish_kernel,
        "finish",
        [VM, VM, VM],
        [(sds((leaf, width), F32), VM), (sds((3, SUB, width), BF), VM)],
        flops=2 * leaf * 256 * width,
        nbytes=leaf * width * 8 + leaf * 512 + TREE * COLS * 512,
    )(back_got, back, bare)
    return leaf_solution[None, None], sep_solution[None, None]


def solution(mesh):
    leaves, fronts = mesh.shape["leaf"], mesh.shape["front"]
    grid = Mesh(
        np.asarray(mesh.devices).reshape(leaves // TREE, TREE, fronts), ("tree", "peer", "front")
    )
    leaf = ("tree", "peer")
    in_specs = (
        P(leaf, "front", None, None),
        P(leaf, "front", None),
        P(leaf, "front", None),
        P(leaf, "front", None, None, None),
        P(leaf, "front", None, None),
        P(leaf, "front", None, None, None),
        P(leaf, "front", None, None),
        P(leaf, "front", None, None),
        P(leaf, "front", None, None, None),
        P(leaf, "front", None, None),
    )
    out_specs = (P(leaf, "front", None, None), P(leaf, "front", None, None, None))
    return jax.shard_map(
        on_device, mesh=grid, in_specs=in_specs, out_specs=out_specs, check_vma=False
    )
```

```python
import jax
import jax.numpy as jnp
import numpy as np
from jax import lax
from jax.experimental import pallas as pl
from jax.experimental.pallas import tpu as pltpu
from jax.sharding import Mesh, PartitionSpec as P

BF = jnp.bfloat16
F32 = jnp.float32
SUB = 16
TREE = 8
COLS = 32
VMEM_CAP = 40 * 1024 * 1024
VMEM_ALL = 62 * 1024 * 1024

NN = (((1,), (0,)), ((), ()))
NT = (((1,), (1,)), ((), ()))
TN = (((0,), (0,)), ((), ()))


def dot(a, b, dims=NN):
    return lax.dot_general(a, b, dims, preferred_element_type=F32)


def lane_ids(rows, cols):
    return lax.broadcasted_iota(jnp.int32, (rows, cols), 1)


def row_ids(rows, cols):
    return lax.broadcasted_iota(jnp.int32, (rows, cols), 0)


def hot(mask):
    return jnp.where(mask, 1.0, 0.0).astype(BF)


VM = pl.BlockSpec(memory_space=pltpu.VMEM)
SM = pl.BlockSpec(memory_space=pltpu.SMEM)
HB = pl.BlockSpec(memory_space=pltpu.HBM)
DMA = pltpu.SemaphoreType.DMA


def call(kernel, name, ins, outs, scratch=(), flops=0, nbytes=0, vmem=VMEM_CAP):
    return pl.pallas_call(
        kernel,
        out_shape=[shape for shape, _ in outs],
        in_specs=list(ins),
        out_specs=[spec for _, spec in outs],
        scratch_shapes=list(scratch),
        compiler_params=pltpu.CompilerParams(vmem_limit_bytes=vmem),
        cost_estimate=pl.CostEstimate(flops=flops, bytes_accessed=nbytes, transcendentals=0),
        name=name,
    )


def fetch(source, target, sem):
    copy = pltpu.make_async_copy(source, target, sem)
    copy.start()
    return copy


def send_kernel(keep, pad, order_hbm, rhs_hbm, out_hbm, order_ref, rhs_ref, picked_ref, out_ref, sems):
    rows, width = rhs_ref.shape
    order_in = fetch(order_hbm, order_ref, sems.at[0])
    rhs_in = fetch(rhs_hbm, rhs_ref, sems.at[1])
    tail = picked_ref.shape[0] - rows
    picked_ref[rows:, :] = jnp.zeros((tail, width), F32)
    lanes = lane_ids(128, 128).astype(F32).astype(BF)
    one, zero = jnp.ones((128, 128), BF), jnp.zeros((128, 128), BF)
    order_in.wait()
    hots = []
    for at in range(0, rows, 128):
        ids = jnp.broadcast_to(order_ref[:, at : at + 128], (128, 128)).T.astype(F32)
        tiles = [jnp.where(lanes == (ids - base).astype(BF), one, zero) for base in range(0, rows, 128)]
        hots.append(jnp.concatenate(tiles, axis=1))
    rhs_in.wait()
    picked_ref[0:rows, :] = dot(jnp.concatenate(hots, axis=0), rhs_ref[...])
    for owner in range(rows // keep):
        out_ref[owner * pad : (owner + 1) * pad, :] = picked_ref[
            owner * keep : owner * keep + pad, :
        ].astype(BF)
    fetch(out_ref, out_hbm, sems.at[2]).wait()


def column_cuts(leaf):
    cuts, base = [], 0
    for low in range(0, leaf, 256):
        cuts.append((low, min(low + 256, leaf), base))
        base += leaf - low
    return cuts


def factor_kernel(
    place_ref, rows_ref, srow_ref, inv_ref, panels_hbm, sinv_hbm, span_hbm, srhs_hbm,
    push_ref, back_ref, side_ref, packed_hbm, panels_ref, sinv_ref, span_ref, srhs_ref, sems,
):
    moves = [
        fetch(sinv_hbm, sinv_ref, sems.at[0]),
        fetch(span_hbm, span_ref, sems.at[1]),
        fetch(srhs_hbm, srhs_ref, sems.at[2]),
        fetch(panels_hbm, panels_ref, sems.at[3]),
    ]
    leaf = inv_ref.shape[0]
    slots = place_ref.shape[1]
    upd = rows_ref.shape[2]
    cuts = column_cuts(leaf)
    leaving = [
        fetch(
            inv_ref.at[low:leaf, low:high],
            packed_hbm.at[base : base + leaf - low, 0 : high - low],
            sems.at[4 + at],
        )
        for at, (low, high, base) in enumerate(cuts)
    ]
    spread = hot(row_ids(leaf, slots) == place_ref[...])
    for move in moves:
        move.wait()
    product = [dot(panels_ref[:, low:], inv_ref[low:, low:high]) for low, high, _ in cuts]
    product = jnp.concatenate(product, axis=1)
    push_ref[...] = dot(product.astype(BF), spread).astype(BF)
    padded = jnp.concatenate([product, jnp.zeros((256 - product.shape[0], leaf), F32)], axis=0)
    back_ref[...] = padded.T.astype(BF)
    cols = sinv_ref.shape[1]
    lane = lane_ids(cols, 256)
    source = jnp.where(
        lane < 128, lane + 96, jnp.where(lane < 192, lane - 96, jnp.where(lane < 224, lane - 192, -1))
    )
    side_ref[0:32, :] = dot(sinv_ref[...], hot(row_ids(cols, 256) == source)).astype(BF)
    lists = [srow_ref[pair].astype(F32) for pair in range(3)]
    lists += [rows_ref[level].astype(F32) for level in range(3)]
    lists = jnp.concatenate(lists + [jnp.zeros((SUB - 6, upd), F32)], axis=0)
    flipped = [span_ref[pair].astype(F32) for pair in range(3)]
    side_ref[32:48, :] = jnp.concatenate(flipped + [lists], axis=1).astype(BF)
    for level in range(3):
        side_ref[48 + level * SUB : 64 + level * SUB, :] = srhs_ref[level]
    side_ref[96:112, :] = jnp.zeros((SUB, 256), BF)
    for copy in leaving:
        copy.wait()


def push_kernel(recv_ref, push_ref, side_ref, out_ref):
    sums = dot(push_ref[...], recv_ref[...])
    rows = jnp.concatenate([sums, side_ref[48:112, :].astype(F32)], axis=0)
    turned = rows.T.astype(BF)
    meta = side_ref[0:48, :]
    for peer in range(TREE):
        out_ref[peer, 0:32, :] = turned[peer * COLS : (peer + 1) * COLS, :]
        out_ref[peer, 32:80, :] = meta


def forward_kernel(leaf, place_ref, recv_ref, packed_ref, y_ref):
    slots = place_ref.shape[1]
    spread = hot(row_ids(leaf, slots) == place_ref[...])
    owned = dot(spread, recv_ref[...]).T.astype(BF)
    cuts = column_cuts(leaf)
    y_t = []
    for low, high, _ in cuts:
        total = None
        for left, right, base in cuts:
            if left <= low:
                rows = slice(base + low - left, base + high - left)
                term = dot(owned[:, left:right], packed_ref[rows, 0 : right - left], NT)
                total = term if total is None else total + term
        y_t.append(total)
    y_ref[...] = jnp.concatenate(y_t, axis=1).astype(BF)


def backward_kernel(y_ref, packed_ref, out_ref):
    leaf = out_ref.shape[0]
    cuts = column_cuts(leaf)
    y_t = y_ref[...]
    bare_t = [
        dot(y_t[:, low:], packed_ref[base : base + leaf - low, 0 : high - low])
        for low, high, base in cuts
    ]
    out_ref[...] = jnp.concatenate(bare_t, axis=1).T


def hot_at(where, rows):
    cols = where.shape[1]
    here = row_ids(rows, cols).astype(F32).astype(BF)
    there = jnp.broadcast_to(where, (SUB, cols)).astype(BF)
    there = jnp.concatenate([there] * (rows // SUB), axis=0)
    return jnp.where(here == there, jnp.ones((rows, cols), BF), jnp.zeros((rows, cols), BF))


def turn(value, shift):
    shift = shift % 128
    return pltpu.roll(value, shift, 1) if shift else value


def tree_kernel(
    front_ref, got_ref, other_ref, bare_hbm, out_ref,
    e0_ref, e1_ref, e2_ref, a01_ref, a02_ref, a12_ref, spots_ref,
):
    front = front_ref[0]
    first = front == 0
    sides = (got_ref, other_ref)
    lane = lane_ids(32, 128)
    none = jnp.zeros((32, 128), BF)
    for peer in range(TREE):
        rows = slice(peer * 32, (peer + 1) * 32)
        mine = got_ref[peer, 32:64, :].astype(F32)
        theirs = other_ref[peer, 32:64, :].astype(F32)
        left = jnp.where(first, mine, theirs)
        right = jnp.where(first, theirs, mine)
        e2_ref[rows, 0:128] = left[:, 0:128].astype(BF)
        e2_ref[rows, 128:256] = right[:, 0:128].astype(BF)
        left, right = left[:, 128:256], right[:, 128:256]
        low1 = jnp.where(lane < 64, left, turn(right, 64))
        inside = (lane >= 64) & (lane < 96)
        to = ((peer // 2) % 2) * 64
        low0 = turn(jnp.where(inside, left, 0.0), to - 64)
        low0 = low0 + turn(jnp.where(inside, right, 0.0), to + 32 - 64)
        tile = peer // 4
        for ref, low in ((e1_ref, low1), (e0_ref, low0)):
            ref[rows, tile * 128 : (tile + 1) * 128] = low.astype(BF)
            ref[rows, (1 - tile) * 128 : (2 - tile) * 128] = none
    for side, table in enumerate(sides):
        for peer in range(TREE):
            at = peer * 2 * SUB + (front ^ side) * SUB
            rows = pl.ds(pl.multiple_of(at, SUB), SUB)
            for pair, ref in enumerate((a01_ref, a02_ref, a12_ref)):
                where = table[peer, 64 + pair : 65 + pair, 192:256].astype(F32)
                if pair == 0:
                    where = where + float(peer // 4 * 128)
                flipped = table[peer, 64:80, pair * 64 : (pair + 1) * 64]
                ref[rows, :] = dot(flipped, hot_at(where, 256), NT).astype(BF)
    for level in range(3):
        for quad in range(4):
            parts = []
            for peer in range(quad % 2 * 4, quad % 2 * 4 + 4):
                where = sides[quad // 2][peer, 67 + level : 68 + level, 192:256].astype(F32)
                parts.append(where + (peer // 2 * 64.0, peer // 4 * 128.0, 0.0)[level])
            spots_ref[level * 4 + quad] = hot_at(jnp.concatenate(parts, axis=1), 256)
    lane = lane_ids(COLS, 128)
    half = lane < 64
    sums = []
    for level in range(3):
        begin = 64 + level * SUB
        inside = (lane >= begin) & (lane < begin + SUB)
        tiles = []
        for tile in range(2):
            totals = []
            for table in sides:
                total = jnp.zeros((COLS, 128), F32)
                for at in range(4):
                    piece = table[tile * 4 + at, 0:32, 128:256].astype(F32)
                    total = total + turn(jnp.where(inside, piece, 0.0), at * 32 - begin)
                totals.append(total)
            mine, theirs = totals
            left = jnp.where(first, mine, theirs)
            right = jnp.where(first, theirs, mine)
            tiles.append(left + turn(right, SUB))
        rest = jnp.concatenate(tiles, axis=1)
        tile = slice(level // 2 * 128, level // 2 * 128 + 128)
        for quad in range(4):
            table = sides[quad // 2]
            halves = []
            for pair in range(2):
                peer = quad % 2 * 4 + pair * 2
                left = table[peer, 0:32, tile].astype(F32)
                right = table[peer + 1, 0:32, tile].astype(F32)
                if level == 1:
                    halves.append(jnp.where(half, turn(left, 64), right))
                else:
                    halves.append(jnp.where(half, left, turn(right, 64)))
            moved = jnp.concatenate(halves, axis=1).astype(BF)
            rest = rest - dot(moved, spots_ref[level * 4 + quad], NT)
        sums.append(rest)
    r0, r1, r2 = sums
    e0, e1, e2 = e0_ref[...], e1_ref[...], e2_ref[...]
    a01, a02, a12 = a01_ref[...], a02_ref[...], a12_ref[...]
    c01 = dot(e0, a01, TN).astype(BF)
    c02 = dot(e0, a02, TN).astype(BF)
    c12 = dot(e1, a12, TN).astype(BF)
    g0 = dot(e0, e0, TN).astype(BF)
    g1 = dot(e1, e1, TN).astype(BF)
    g2 = dot(e2, e2, TN).astype(BF)
    r0 = r0.astype(BF)
    r1 = (r1 - dot(r0, c01)).astype(BF)
    r2 = (r2 - dot(r0, c02) - dot(r1, c12)).astype(BF)
    x2 = dot(r2, g2).astype(BF)
    x1 = (dot(r1, g1) - dot(x2, c12, NT)).astype(BF)
    x0 = (dot(r0, g0) - dot(x2, c02, NT) - dot(x1, c01, NT)).astype(BF)
    solved = (x0, x1, x2)
    own = []
    for level in range(3):
        for tile in range(2):
            piece = solved[level][:, tile * 128 : (tile + 1) * 128].astype(F32)
            own.append(jnp.where(first, piece, turn(piece, -SUB)))
    for quad in range(2):
        picks = [dot(solved[level], spots_ref[level * 4 + quad]) for level in range(3)]
        for at in range(4):
            peer = quad * 4 + at
            part = slice(at // 2 * 128, at // 2 * 128 + 128)
            p0, p1, p2 = [pick[:, part] for pick in picks]
            if at % 2:
                p0, p2 = turn(p0, 64), turn(p2, 64)
            else:
                p1 = turn(p1, 64)
            out_ref[peer, :, 0:128] = jnp.where(half, p0, p1).astype(BF)
            rest = jnp.where(half, p2, 0.0)
            for level in range(3):
                begin = 64 + level * SUB
                piece = turn(own[level * 2 + quad], begin - at * 32)
                rest = jnp.where((lane >= begin) & (lane < begin + SUB), piece, rest)
            out_ref[peer, :, 128:256] = rest.astype(BF)


def finish_kernel(got_ref, back_ref, leaf_ref, out_ref, sep_ref):
    table = got_ref[...].reshape(256, 256)
    out_ref[...] = leaf_ref[...] - dot(back_ref[...], table, NT)
    pick = hot(lane_ids(48, 256) == row_ids(48, 256) + 192)
    rows = dot(pick, table, NT).astype(BF)
    for level in range(3):
        sep_ref[level] = rows[level * SUB : (level + 1) * SUB, :]


def on_device(
    rhs_parts,
    send_order,
    recv_place,
    sep_rhs,
    leaf_inv,
    leaf_panels,
    leaf_rows,
    sep_inv,
    sep_panels,
    sep_rows,
):
    owners = lax.axis_size("tree") * lax.axis_size("peer")
    rhs = rhs_parts[0, 0]
    leaf, width = rhs.shape
    inv = leaf_inv[0, 0]
    panels = leaf_panels[0, 0].reshape(-1, leaf)
    keep = leaf // owners
    pad = -(-keep // 8) * 8
    slots = owners * pad
    sds = jax.ShapeDtypeStruct

    (sent,) = call(
        lambda *refs: send_kernel(keep, pad, *refs),
        "send_rows",
        [HB, HB],
        [(sds((slots, width), BF), HB)],
        [
            pltpu.VMEM((1, leaf), jnp.int32),
            pltpu.VMEM((leaf, width), BF),
            pltpu.VMEM((-(-(leaf - keep + pad) // 8) * 8 + 8, width), F32),
            pltpu.VMEM((slots, width), BF),
            DMA((3,)),
        ],
        flops=2 * leaf * leaf * width,
        nbytes=2 * leaf * width * 2,
        vmem=VMEM_ALL,
    )(send_order[0], rhs)
    recv = lax.all_to_all(
        sent.reshape(owners, pad, width), ("tree", "peer"), split_axis=0, concat_axis=0, tiled=True
    ).reshape(slots, width)

    place = jnp.pad(
        recv_place[0, 0].reshape(owners, keep), ((0, 0), (0, pad - keep)), constant_values=-1
    ).reshape(1, slots)
    span = jnp.swapaxes(sep_panels[0, 0], 1, 2)
    packed_rows = sum(leaf - low for low, _, _ in column_cuts(leaf))
    push, back, side, packed = call(
        factor_kernel,
        "factor_products",
        [VM, VM, VM, VM, HB, HB, HB, HB],
        [
            (sds((192, slots), BF), VM),
            (sds((leaf, 256), BF), VM),
            (sds((112, 256), BF), VM),
            (sds((packed_rows, 256), BF), HB),
        ],
        [
            pltpu.VMEM(panels.shape, BF),
            pltpu.VMEM(sep_inv.shape[2:], BF),
            pltpu.VMEM(span.shape, BF),
            pltpu.VMEM(sep_rhs.shape[2:], BF),
            DMA((4 + len(column_cuts(leaf)),)),
        ],
        flops=2 * 192 * leaf * (leaf + slots),
        nbytes=2 * leaf * leaf + 2 * 192 * slots + 2 * 256 * leaf,
    )(
        place,
        leaf_rows[0, 0][:, None, :],
        sep_rows[0, 0][:, None, :],
        inv,
        panels,
        sep_inv[0, 0],
        span,
        sep_rhs[0, 0],
    )
    (chunks,) = call(
        push_kernel,
        "push_updates",
        [VM, VM, VM],
        [(sds((TREE, 80, 256), BF), VM)],
        flops=2 * 192 * slots * width,
        nbytes=2 * slots * (192 + width) + TREE * 80 * 512,
    )(recv, push, side)
    got = lax.all_to_all(chunks, "peer", split_axis=0, concat_axis=0, tiled=True)
    (leaf_y,) = call(
        lambda *refs: forward_kernel(leaf, *refs),
        "leaf_forward",
        [VM, VM, VM],
        [(sds((width, leaf), BF), VM)],
        flops=2 * leaf * width * (leaf + slots),
        nbytes=2 * leaf * leaf + 4 * slots * width,
    )(place, recv, packed)
    got, leaf_y = lax.optimization_barrier((got, leaf_y))
    other = lax.ppermute(got, "front", [(0, 1), (1, 0)])
    front = lax.axis_index("front").astype(jnp.int32).reshape(1)
    (bare,) = call(
        backward_kernel,
        "leaf_backward",
        [VM, VM],
        [(sds((leaf, width), F32), VM)],
        flops=2 * leaf * width * leaf,
        nbytes=2 * leaf * leaf + 6 * leaf * width,
    )(leaf_y, packed)
    square = pltpu.VMEM((256, 256), BF)
    (solved,) = call(
        tree_kernel,
        "separator_tree",
        [SM, VM, VM, pl.BlockSpec(memory_space=pl.ANY)],
        [(sds((TREE, COLS, 256), BF), VM)],
        [square] * 6 + [pltpu.VMEM((12, 256, 256), BF)],
        flops=2 * 32 * 256 * 256 * 30 + 2 * 48 * 16 * 64 * 256,
        nbytes=TREE * 192 * 512,
    )(front, got, other, bare)
    back_got = lax.all_to_all(solved, "peer", split_axis=0, concat_axis=0, tiled=True)

    leaf_solution, sep_solution = call(
        finish_kernel,
        "finish",
        [VM, VM, VM],
        [(sds((leaf, width), F32), VM), (sds((3, SUB, width), BF), VM)],
        flops=2 * leaf * 256 * width,
        nbytes=leaf * width * 8 + leaf * 512 + TREE * COLS * 512,
    )(back_got, back, bare)
    return leaf_solution[None, None], sep_solution[None, None]


def solution(mesh):
    leaves, fronts = mesh.shape["leaf"], mesh.shape["front"]
    grid = Mesh(
        np.asarray(mesh.devices).reshape(leaves // TREE, TREE, fronts), ("tree", "peer", "front")
    )
    leaf = ("tree", "peer")
    in_specs = (
        P(leaf, "front", None, None),
        P(leaf, "front", None),
        P(leaf, "front", None),
        P(leaf, "front", None, None, None),
        P(leaf, "front", None, None),
        P(leaf, "front", None, None, None),
        P(leaf, "front", None, None),
        P(leaf, "front", None, None),
        P(leaf, "front", None, None, None),
        P(leaf, "front", None, None),
    )
    out_specs = (P(leaf, "front", None, None), P(leaf, "front", None, None, None))
    return jax.shard_map(
        on_device, mesh=grid, in_specs=in_specs, out_specs=out_specs, check_vma=False
    )
```

```python
import jax
import jax.numpy as jnp
import numpy as np
from jax import lax
from jax.experimental import pallas as pl
from jax.experimental.pallas import tpu as pltpu
from jax.sharding import Mesh, PartitionSpec as P

BF = jnp.bfloat16
F32 = jnp.float32
SUB = 16
TREE = 8
COLS = 32
VMEM_CAP = 40 * 1024 * 1024
VMEM_ALL = 62 * 1024 * 1024

NN = (((1,), (0,)), ((), ()))
NT = (((1,), (1,)), ((), ()))
TN = (((0,), (0,)), ((), ()))


def dot(a, b, dims=NN):
    return lax.dot_general(a, b, dims, preferred_element_type=F32)


def lane_ids(rows, cols):
    return lax.broadcasted_iota(jnp.int32, (rows, cols), 1)


def row_ids(rows, cols):
    return lax.broadcasted_iota(jnp.int32, (rows, cols), 0)


def hot(mask):
    return jnp.where(mask, 1.0, 0.0).astype(BF)


VM = pl.BlockSpec(memory_space=pltpu.VMEM)
SM = pl.BlockSpec(memory_space=pltpu.SMEM)
HB = pl.BlockSpec(memory_space=pltpu.HBM)
DMA = pltpu.SemaphoreType.DMA


def call(kernel, name, ins, outs, scratch=(), flops=0, nbytes=0, vmem=VMEM_CAP):
    return pl.pallas_call(
        kernel,
        out_shape=[shape for shape, _ in outs],
        in_specs=list(ins),
        out_specs=[spec for _, spec in outs],
        scratch_shapes=list(scratch),
        compiler_params=pltpu.CompilerParams(vmem_limit_bytes=vmem),
        cost_estimate=pl.CostEstimate(flops=flops, bytes_accessed=nbytes, transcendentals=0),
        name=name,
    )


def fetch(source, target, sem):
    copy = pltpu.make_async_copy(source, target, sem)
    copy.start()
    return copy


def send_kernel(
    keep, tall, order_hbm, rhs_hbm, out_hbm, order_ref, rhs_ref, picked_ref, stage_ref, out_ref, sems
):
    rows, width = rhs_ref.shape
    half = width // 2
    order_in = fetch(order_hbm, order_ref, sems.at[0])
    rhs_in = fetch(rhs_hbm, rhs_ref, sems.at[1])
    tail = picked_ref.shape[0] - rows
    picked_ref[rows:, :] = jnp.zeros((tail, width), F32)
    lanes = lane_ids(128, 128).astype(F32).astype(BF)
    one, zero = jnp.ones((128, 128), BF), jnp.zeros((128, 128), BF)
    order_in.wait()
    hots = []
    for at in range(0, rows, 128):
        ids = jnp.broadcast_to(order_ref[:, at : at + 128], (128, 128)).T.astype(F32)
        tiles = [jnp.where(lanes == (ids - base).astype(BF), one, zero) for base in range(0, rows, 128)]
        hots.append(jnp.concatenate(tiles, axis=1))
    rhs_in.wait()
    picked_ref[0:rows, :] = dot(jnp.concatenate(hots, axis=0), rhs_ref[...])
    span = -(-keep // 8) * 8
    for owner in range(rows // keep):
        source = slice(owner * keep, owner * keep + span)
        base = owner * tall
        stage_ref[base : base + span, :] = picked_ref[source, 0:half]
        stage_ref[base + keep : base + keep + span, :] = picked_ref[source, half:width]
    out_ref[...] = stage_ref[0 : out_ref.shape[0], :].astype(BF)
    fetch(out_ref, out_hbm, sems.at[2]).wait()


def side_by_side(keep, tall, recv_ref, wide_ref):
    sent = recv_ref.shape[0]
    span = wide_ref.shape[0] - sent
    wide_ref[0:sent, :] = recv_ref[...].astype(F32)
    wide_ref[sent:, :] = jnp.zeros((span, wide_ref.shape[1]), F32)
    rows = []
    for base in range(0, sent, tall):
        left = wide_ref[base : base + span, :]
        right = wide_ref[base + keep : base + keep + span, :]
        rows.append(jnp.concatenate([left, right], axis=1))
    return jnp.concatenate(rows, axis=0).astype(BF)


def column_cuts(leaf):
    cuts, base = [], 0
    for low in range(0, leaf, 256):
        cuts.append((low, min(low + 256, leaf), base))
        base += leaf - low
    return cuts


def factor_kernel(
    place_ref, rows_ref, srow_ref, inv_ref, panels_hbm, sinv_hbm, span_hbm, srhs_hbm,
    push_ref, back_ref, side_ref, packed_hbm, panels_ref, sinv_ref, span_ref, srhs_ref, sems,
):
    moves = [
        fetch(sinv_hbm, sinv_ref, sems.at[0]),
        fetch(span_hbm, span_ref, sems.at[1]),
        fetch(srhs_hbm, srhs_ref, sems.at[2]),
        fetch(panels_hbm, panels_ref, sems.at[3]),
    ]
    leaf = inv_ref.shape[0]
    slots = place_ref.shape[1]
    upd = rows_ref.shape[2]
    cuts = column_cuts(leaf)
    leaving = [
        fetch(
            inv_ref.at[low:leaf, low:high],
            packed_hbm.at[base : base + leaf - low, 0 : high - low],
            sems.at[4 + at],
        )
        for at, (low, high, base) in enumerate(cuts)
    ]
    spread = hot(row_ids(leaf, slots) == place_ref[...])
    for move in moves:
        move.wait()
    product = [dot(panels_ref[:, low:], inv_ref[low:, low:high]) for low, high, _ in cuts]
    product = jnp.concatenate(product, axis=1)
    push_ref[0:192, :] = dot(product.astype(BF), spread).astype(BF)
    padded = jnp.concatenate([product, jnp.zeros((256 - product.shape[0], leaf), F32)], axis=0)
    back_ref[...] = padded.T.astype(BF)
    cols = sinv_ref.shape[1]
    lane = lane_ids(cols, 256)
    source = jnp.where(
        lane < 128, lane + 96, jnp.where(lane < 192, lane - 96, jnp.where(lane < 224, lane - 192, -1))
    )
    side_ref[0:32, :] = dot(sinv_ref[...], hot(row_ids(cols, 256) == source)).astype(BF)
    lists = [srow_ref[pair].astype(F32) for pair in range(3)]
    lists += [rows_ref[level].astype(F32) for level in range(3)]
    lists = jnp.concatenate(lists + [jnp.zeros((SUB - 6, upd), F32)], axis=0)
    flipped = [span_ref[pair].astype(F32) for pair in range(3)]
    side_ref[32:48, :] = jnp.concatenate(flipped + [lists], axis=1).astype(BF)
    for level in range(3):
        side_ref[48 + level * SUB : 64 + level * SUB, :] = srhs_ref[level]
    side_ref[96:112, :] = jnp.zeros((SUB, 256), BF)
    for copy in leaving:
        copy.wait()


def push_kernel(keep, tall, recv_ref, push_ref, side_ref, out_ref, wide_ref):
    sums = dot(push_ref[0:192, :], side_by_side(keep, tall, recv_ref, wide_ref))
    rows = jnp.concatenate([sums, side_ref[48:112, :].astype(F32)], axis=0)
    turned = rows.T.astype(BF)
    meta = side_ref[0:48, :]
    for peer in range(TREE):
        out_ref[peer, 0:32, :] = turned[peer * COLS : (peer + 1) * COLS, :]
        out_ref[peer, 32:80, :] = meta


def forward_kernel(leaf, keep, tall, place_ref, recv_ref, packed_ref, y_ref, wide_ref):
    slots = place_ref.shape[1]
    spread = hot(row_ids(leaf, slots) == place_ref[...])
    owned = dot(spread, side_by_side(keep, tall, recv_ref, wide_ref)).T.astype(BF)
    cuts = column_cuts(leaf)
    y_t = []
    for low, high, _ in cuts:
        total = None
        for left, right, base in cuts:
            if left <= low:
                rows = slice(base + low - left, base + high - left)
                term = dot(owned[:, left:right], packed_ref[rows, 0 : right - left], NT)
                total = term if total is None else total + term
        y_t.append(total)
    y_ref[...] = jnp.concatenate(y_t, axis=1).astype(BF)


def backward_kernel(y_ref, packed_ref, out_ref):
    leaf = out_ref.shape[0]
    cuts = column_cuts(leaf)
    y_t = y_ref[...]
    bare_t = [
        dot(y_t[:, low:], packed_ref[base : base + leaf - low, 0 : high - low])
        for low, high, base in cuts
    ]
    out_ref[...] = jnp.concatenate(bare_t, axis=1).T


def hot_at(where, rows):
    cols = where.shape[1]
    here = row_ids(rows, cols).astype(F32).astype(BF)
    there = jnp.broadcast_to(where, (SUB, cols)).astype(BF)
    there = jnp.concatenate([there] * (rows // SUB), axis=0)
    return jnp.where(here == there, jnp.ones((rows, cols), BF), jnp.zeros((rows, cols), BF))


def turn(value, shift):
    shift = shift % 128
    return pltpu.roll(value, shift, 1) if shift else value


def tree_kernel(
    front_ref, got_ref, other_ref, bare_hbm, out_ref,
    e0_ref, e1_ref, e2_ref, a01_ref, a02_ref, a12_ref, spots_ref,
):
    front = front_ref[0]
    first = front == 0
    sides = (got_ref, other_ref)
    lane = lane_ids(32, 128)
    none = jnp.zeros((32, 128), BF)
    for peer in range(TREE):
        rows = slice(peer * 32, (peer + 1) * 32)
        mine = got_ref[peer, 32:64, :].astype(F32)
        theirs = other_ref[peer, 32:64, :].astype(F32)
        left = jnp.where(first, mine, theirs)
        right = jnp.where(first, theirs, mine)
        e2_ref[rows, 0:128] = left[:, 0:128].astype(BF)
        e2_ref[rows, 128:256] = right[:, 0:128].astype(BF)
        left, right = left[:, 128:256], right[:, 128:256]
        low1 = jnp.where(lane < 64, left, turn(right, 64))
        inside = (lane >= 64) & (lane < 96)
        to = ((peer // 2) % 2) * 64
        low0 = turn(jnp.where(inside, left, 0.0), to - 64)
        low0 = low0 + turn(jnp.where(inside, right, 0.0), to + 32 - 64)
        tile = peer // 4
        for ref, low in ((e1_ref, low1), (e0_ref, low0)):
            ref[rows, tile * 128 : (tile + 1) * 128] = low.astype(BF)
            ref[rows, (1 - tile) * 128 : (2 - tile) * 128] = none
    for side, table in enumerate(sides):
        for peer in range(TREE):
            at = peer * 2 * SUB + (front ^ side) * SUB
            rows = pl.ds(pl.multiple_of(at, SUB), SUB)
            for pair, ref in enumerate((a01_ref, a02_ref, a12_ref)):
                where = table[peer, 64 + pair : 65 + pair, 192:256].astype(F32)
                if pair == 0:
                    where = where + float(peer // 4 * 128)
                flipped = table[peer, 64:80, pair * 64 : (pair + 1) * 64]
                ref[rows, :] = dot(flipped, hot_at(where, 256), NT).astype(BF)
    for level in range(3):
        for quad in range(4):
            parts = []
            for peer in range(quad % 2 * 4, quad % 2 * 4 + 4):
                where = sides[quad // 2][peer, 67 + level : 68 + level, 192:256].astype(F32)
                parts.append(where + (peer // 2 * 64.0, peer // 4 * 128.0, 0.0)[level])
            spots_ref[level * 4 + quad] = hot_at(jnp.concatenate(parts, axis=1), 256)
    lane = lane_ids(COLS, 128)
    half = lane < 64
    sums = []
    for level in range(3):
        begin = 64 + level * SUB
        inside = (lane >= begin) & (lane < begin + SUB)
        tiles = []
        for tile in range(2):
            totals = []
            for table in sides:
                total = jnp.zeros((COLS, 128), F32)
                for at in range(4):
                    piece = table[tile * 4 + at, 0:32, 128:256].astype(F32)
                    total = total + turn(jnp.where(inside, piece, 0.0), at * 32 - begin)
                totals.append(total)
            mine, theirs = totals
            left = jnp.where(first, mine, theirs)
            right = jnp.where(first, theirs, mine)
            tiles.append(left + turn(right, SUB))
        rest = jnp.concatenate(tiles, axis=1)
        tile = slice(level // 2 * 128, level // 2 * 128 + 128)
        for quad in range(4):
            table = sides[quad // 2]
            halves = []
            for pair in range(2):
                peer = quad % 2 * 4 + pair * 2
                left = table[peer, 0:32, tile].astype(F32)
                right = table[peer + 1, 0:32, tile].astype(F32)
                if level == 1:
                    halves.append(jnp.where(half, turn(left, 64), right))
                else:
                    halves.append(jnp.where(half, left, turn(right, 64)))
            moved = jnp.concatenate(halves, axis=1).astype(BF)
            rest = rest - dot(moved, spots_ref[level * 4 + quad], NT)
        sums.append(rest)
    r0, r1, r2 = sums
    e0, e1, e2 = e0_ref[...], e1_ref[...], e2_ref[...]
    a01, a02, a12 = a01_ref[...], a02_ref[...], a12_ref[...]
    c01 = dot(e0, a01, TN).astype(BF)
    c02 = dot(e0, a02, TN).astype(BF)
    c12 = dot(e1, a12, TN).astype(BF)
    g0 = dot(e0, e0, TN).astype(BF)
    g1 = dot(e1, e1, TN).astype(BF)
    g2 = dot(e2, e2, TN).astype(BF)
    r0 = r0.astype(BF)
    r1 = (r1 - dot(r0, c01)).astype(BF)
    r2 = (r2 - dot(r0, c02) - dot(r1, c12)).astype(BF)
    x2 = dot(r2, g2).astype(BF)
    x1 = (dot(r1, g1) - dot(x2, c12, NT)).astype(BF)
    x0 = (dot(r0, g0) - dot(x2, c02, NT) - dot(x1, c01, NT)).astype(BF)
    solved = (x0, x1, x2)
    own = []
    for level in range(3):
        for tile in range(2):
            piece = solved[level][:, tile * 128 : (tile + 1) * 128].astype(F32)
            own.append(jnp.where(first, piece, turn(piece, -SUB)))
    for quad in range(2):
        picks = [dot(solved[level], spots_ref[level * 4 + quad]) for level in range(3)]
        for at in range(4):
            peer = quad * 4 + at
            part = slice(at // 2 * 128, at // 2 * 128 + 128)
            p0, p1, p2 = [pick[:, part] for pick in picks]
            if at % 2:
                p0, p2 = turn(p0, 64), turn(p2, 64)
            else:
                p1 = turn(p1, 64)
            out_ref[peer, :, 0:128] = jnp.where(half, p0, p1).astype(BF)
            rest = jnp.where(half, p2, 0.0)
            for level in range(3):
                begin = 64 + level * SUB
                piece = turn(own[level * 2 + quad], begin - at * 32)
                rest = jnp.where((lane >= begin) & (lane < begin + SUB), piece, rest)
            out_ref[peer, :, 128:256] = rest.astype(BF)


def finish_kernel(got_ref, back_ref, leaf_ref, out_ref, sep_ref):
    table = got_ref[...].reshape(256, 256)
    out_ref[...] = leaf_ref[...] - dot(back_ref[...], table, NT)
    pick = hot(lane_ids(48, 256) == row_ids(48, 256) + 192)
    rows = dot(pick, table, NT).astype(BF)
    for level in range(3):
        sep_ref[level] = rows[level * SUB : (level + 1) * SUB, :]


def on_device(
    rhs_parts,
    send_order,
    recv_place,
    sep_rhs,
    leaf_inv,
    leaf_panels,
    leaf_rows,
    sep_inv,
    sep_panels,
    sep_rows,
):
    owners = lax.axis_size("tree") * lax.axis_size("peer")
    rhs = rhs_parts[0, 0]
    leaf, width = rhs.shape
    inv = leaf_inv[0, 0]
    panels = leaf_panels[0, 0].reshape(-1, leaf)
    keep = leaf // owners
    half = width // 2
    tall = -(-2 * keep // 8) * 8
    span = -(-keep // 8) * 8
    slots = owners * span
    wide = pltpu.VMEM((owners * tall + span, half), F32)
    sds = jax.ShapeDtypeStruct

    (sent,) = call(
        lambda *refs: send_kernel(keep, tall, *refs),
        "send_rows",
        [HB, HB],
        [(sds((owners * tall, half), BF), HB)],
        [
            pltpu.VMEM((1, leaf), jnp.int32),
            pltpu.VMEM((leaf, width), BF),
            pltpu.VMEM((leaf + 8, width), F32),
            pltpu.VMEM((owners * tall + 8, half), F32),
            pltpu.VMEM((owners * tall, half), BF),
            DMA((3,)),
        ],
        flops=2 * leaf * leaf * width,
        nbytes=2 * leaf * width * 2,
        vmem=VMEM_ALL,
    )(send_order[0], rhs)
    recv = lax.all_to_all(
        sent.reshape(owners, tall, half), ("tree", "peer"), split_axis=0, concat_axis=0, tiled=True
    ).reshape(owners * tall, half)

    place = jnp.pad(
        recv_place[0, 0].reshape(owners, keep), ((0, 0), (0, span - keep)), constant_values=-1
    ).reshape(1, slots)
    span = jnp.swapaxes(sep_panels[0, 0], 1, 2)
    packed_rows = sum(leaf - low for low, _, _ in column_cuts(leaf))
    push, back, side, packed = call(
        factor_kernel,
        "factor_products",
        [VM, VM, VM, VM, HB, HB, HB, HB],
        [
            (sds((320, slots), BF), VM),
            (sds((leaf, 256), BF), VM),
            (sds((112, 256), BF), VM),
            (sds((packed_rows, 256), BF), HB),
        ],
        [
            pltpu.VMEM(panels.shape, BF),
            pltpu.VMEM(sep_inv.shape[2:], BF),
            pltpu.VMEM(span.shape, BF),
            pltpu.VMEM(sep_rhs.shape[2:], BF),
            DMA((4 + len(column_cuts(leaf)),)),
        ],
        flops=2 * 192 * leaf * (leaf + slots),
        nbytes=2 * leaf * leaf + 2 * 192 * slots + 2 * 256 * leaf,
    )(
        place,
        leaf_rows[0, 0][:, None, :],
        sep_rows[0, 0][:, None, :],
        inv,
        panels,
        sep_inv[0, 0],
        span,
        sep_rhs[0, 0],
    )
    (chunks,) = call(
        lambda *refs: push_kernel(keep, tall, *refs),
        "push_updates",
        [VM, VM, VM],
        [(sds((TREE, 80, 256), BF), VM)],
        [wide],
        flops=2 * 192 * slots * width,
        nbytes=2 * slots * (192 + width) + TREE * 80 * 512,
    )(recv, push, side)
    got = lax.all_to_all(chunks, "peer", split_axis=0, concat_axis=0, tiled=True)
    (leaf_y,) = call(
        lambda *refs: forward_kernel(leaf, keep, tall, *refs),
        "leaf_forward",
        [VM, VM, VM],
        [(sds((width, leaf), BF), VM)],
        [wide],
        flops=2 * leaf * width * (leaf + slots),
        nbytes=2 * leaf * leaf + 4 * slots * width,
    )(place, recv, packed)
    got, leaf_y = lax.optimization_barrier((got, leaf_y))
    other = lax.ppermute(got, "front", [(0, 1), (1, 0)])
    front = lax.axis_index("front").astype(jnp.int32).reshape(1)
    (bare,) = call(
        backward_kernel,
        "leaf_backward",
        [VM, VM],
        [(sds((leaf, width), F32), VM)],
        flops=2 * leaf * width * leaf,
        nbytes=2 * leaf * leaf + 6 * leaf * width,
    )(leaf_y, packed)
    square = pltpu.VMEM((256, 256), BF)
    (solved,) = call(
        tree_kernel,
        "separator_tree",
        [SM, VM, VM, pl.BlockSpec(memory_space=pl.ANY)],
        [(sds((TREE, COLS, 256), BF), VM)],
        [square] * 6 + [pltpu.VMEM((12, 256, 256), BF)],
        flops=2 * 32 * 256 * 256 * 30 + 2 * 48 * 16 * 64 * 256,
        nbytes=TREE * 192 * 512,
    )(front, got, other, bare)
    back_got = lax.all_to_all(solved, "peer", split_axis=0, concat_axis=0, tiled=True)

    leaf_solution, sep_solution = call(
        finish_kernel,
        "finish",
        [VM, VM, VM],
        [(sds((leaf, width), F32), VM), (sds((3, SUB, width), BF), VM)],
        flops=2 * leaf * 256 * width,
        nbytes=leaf * width * 8 + leaf * 512 + TREE * COLS * 512,
    )(back_got, back, bare)
    return leaf_solution[None, None], sep_solution[None, None]


def solution(mesh):
    leaves, fronts = mesh.shape["leaf"], mesh.shape["front"]
    grid = Mesh(
        np.asarray(mesh.devices).reshape(leaves // TREE, TREE, fronts), ("tree", "peer", "front")
    )
    leaf = ("tree", "peer")
    in_specs = (
        P(leaf, "front", None, None),
        P(leaf, "front", None),
        P(leaf, "front", None),
        P(leaf, "front", None, None, None),
        P(leaf, "front", None, None),
        P(leaf, "front", None, None, None),
        P(leaf, "front", None, None),
        P(leaf, "front", None, None),
        P(leaf, "front", None, None, None),
        P(leaf, "front", None, None),
    )
    out_specs = (P(leaf, "front", None, None), P(leaf, "front", None, None, None))
    return jax.shard_map(
        on_device, mesh=grid, in_specs=in_specs, out_specs=out_specs, check_vma=False
    )
```

```python
import jax
import jax.numpy as jnp
import numpy as np
from jax import lax
from jax.experimental import pallas as pl
from jax.experimental.pallas import tpu as pltpu
from jax.sharding import Mesh, PartitionSpec as P

BF = jnp.bfloat16
F32 = jnp.float32
SUB = 16
TREE = 8
COLS = 32
VMEM_CAP = 40 * 1024 * 1024
VMEM_ALL = 62 * 1024 * 1024

NN = (((1,), (0,)), ((), ()))
NT = (((1,), (1,)), ((), ()))
TN = (((0,), (0,)), ((), ()))


def dot(a, b, dims=NN):
    return lax.dot_general(a, b, dims, preferred_element_type=F32)


def lane_ids(rows, cols):
    return lax.broadcasted_iota(jnp.int32, (rows, cols), 1)


def row_ids(rows, cols):
    return lax.broadcasted_iota(jnp.int32, (rows, cols), 0)


def hot(mask):
    return jnp.where(mask, 1.0, 0.0).astype(BF)


VM = pl.BlockSpec(memory_space=pltpu.VMEM)
SM = pl.BlockSpec(memory_space=pltpu.SMEM)
HB = pl.BlockSpec(memory_space=pltpu.HBM)
DMA = pltpu.SemaphoreType.DMA


def call(kernel, name, ins, outs, scratch=(), flops=0, nbytes=0, vmem=VMEM_CAP):
    return pl.pallas_call(
        kernel,
        out_shape=[shape for shape, _ in outs],
        in_specs=list(ins),
        out_specs=[spec for _, spec in outs],
        scratch_shapes=list(scratch),
        compiler_params=pltpu.CompilerParams(vmem_limit_bytes=vmem),
        cost_estimate=pl.CostEstimate(flops=flops, bytes_accessed=nbytes, transcendentals=0),
        name=name,
    )


def fetch(source, target, sem):
    copy = pltpu.make_async_copy(source, target, sem)
    copy.start()
    return copy


def send_kernel(
    keep, tall, order_hbm, rhs_hbm, out_hbm, order_ref, rhs_ref, picked_ref, stage_ref, out_ref, sems
):
    rows, width = rhs_ref.shape
    half = width // 2
    order_in = fetch(order_hbm, order_ref, sems.at[0])
    rhs_in = fetch(rhs_hbm, rhs_ref, sems.at[1])
    tail = picked_ref.shape[0] - rows
    picked_ref[rows:, :] = jnp.zeros((tail, width), F32)
    lanes = lane_ids(128, 128).astype(F32).astype(BF)
    one, zero = jnp.ones((128, 128), BF), jnp.zeros((128, 128), BF)
    order_in.wait()
    hots = []
    for at in range(0, rows, 128):
        ids = jnp.broadcast_to(order_ref[:, at : at + 128], (128, 128)).T.astype(F32)
        tiles = [jnp.where(lanes == (ids - base).astype(BF), one, zero) for base in range(0, rows, 128)]
        hots.append(jnp.concatenate(tiles, axis=1))
    rhs_in.wait()
    picked_ref[0:rows, :] = dot(jnp.concatenate(hots, axis=0), rhs_ref[...])
    span = -(-keep // 8) * 8
    for owner in range(rows // keep):
        source = slice(owner * keep, owner * keep + span)
        base = owner * tall
        stage_ref[base : base + span, :] = picked_ref[source, 0:half]
        stage_ref[base + keep : base + keep + span, :] = picked_ref[source, half:width]
    out_ref[...] = stage_ref[0 : out_ref.shape[0], :].astype(BF)
    fetch(out_ref, out_hbm, sems.at[2]).wait()


def side_by_side(keep, tall, recv_ref, wide_ref):
    sent = recv_ref.shape[0]
    span = wide_ref.shape[0] - sent
    wide_ref[0:sent, :] = recv_ref[...].astype(F32)
    wide_ref[sent:, :] = jnp.zeros((span, wide_ref.shape[1]), F32)
    rows = []
    for base in range(0, sent, tall):
        left = wide_ref[base : base + span, :]
        right = wide_ref[base + keep : base + keep + span, :]
        rows.append(jnp.concatenate([left, right], axis=1))
    return jnp.concatenate(rows, axis=0).astype(BF)


def column_cuts(leaf):
    cuts, base = [], 0
    for low in range(0, leaf, 256):
        cuts.append((low, min(low + 256, leaf), base))
        base += leaf - low
    return cuts


def factor_kernel(
    place_ref, rows_ref, srow_ref, inv_ref, panels_hbm, sinv_hbm, span_hbm, srhs_hbm,
    push_ref, back_ref, side_ref, packed_hbm, panels_ref, sinv_ref, span_ref, srhs_ref, sems,
):
    moves = [
        fetch(sinv_hbm, sinv_ref, sems.at[0]),
        fetch(span_hbm, span_ref, sems.at[1]),
        fetch(srhs_hbm, srhs_ref, sems.at[2]),
        fetch(panels_hbm, panels_ref, sems.at[3]),
    ]
    leaf = inv_ref.shape[0]
    slots = place_ref.shape[1]
    upd = rows_ref.shape[2]
    cuts = column_cuts(leaf)
    leaving = [
        fetch(
            inv_ref.at[low:leaf, low:high],
            packed_hbm.at[base : base + leaf - low, 0 : high - low],
            sems.at[4 + at],
        )
        for at, (low, high, base) in enumerate(cuts)
    ]
    spread = hot(row_ids(leaf, slots) == place_ref[...])
    for move in moves:
        move.wait()
    product = [dot(panels_ref[:, low:], inv_ref[low:, low:high]) for low, high, _ in cuts]
    product = jnp.concatenate(product, axis=1)
    push_ref[0:192, :] = dot(product.astype(BF), spread).astype(BF)
    padded = jnp.concatenate([product, jnp.zeros((256 - product.shape[0], leaf), F32)], axis=0)
    back_ref[...] = padded.T.astype(BF)
    cols = sinv_ref.shape[1]
    lane = lane_ids(cols, 256)
    source = jnp.where(
        lane < 128, lane + 96, jnp.where(lane < 192, lane - 96, jnp.where(lane < 224, lane - 192, -1))
    )
    side_ref[0:32, :] = dot(sinv_ref[...], hot(row_ids(cols, 256) == source)).astype(BF)
    lists = [srow_ref[pair].astype(F32) for pair in range(3)]
    lists += [rows_ref[level].astype(F32) for level in range(3)]
    lists = jnp.concatenate(lists + [jnp.zeros((SUB - 6, upd), F32)], axis=0)
    flipped = [span_ref[pair].astype(F32) for pair in range(3)]
    side_ref[32:48, :] = jnp.concatenate(flipped + [lists], axis=1).astype(BF)
    for level in range(3):
        side_ref[48 + level * SUB : 64 + level * SUB, :] = srhs_ref[level]
    side_ref[96:112, :] = jnp.zeros((SUB, 256), BF)
    for copy in leaving:
        copy.wait()


def push_kernel(keep, tall, recv_ref, push_ref, side_ref, out_ref, wide_ref):
    sums = dot(push_ref[0:192, :], side_by_side(keep, tall, recv_ref, wide_ref))
    rows = jnp.concatenate([sums, side_ref[48:112, :].astype(F32)], axis=0)
    turned = rows.T.astype(BF)
    meta = side_ref[0:48, :]
    for peer in range(TREE):
        out_ref[peer, 0:32, :] = turned[peer * COLS : (peer + 1) * COLS, :]
        out_ref[peer, 32:80, :] = meta


def forward_kernel(leaf, keep, tall, place_ref, recv_ref, packed_ref, y_ref, wide_ref):
    slots = place_ref.shape[1]
    spread = hot(row_ids(leaf, slots) == place_ref[...])
    owned = dot(spread, side_by_side(keep, tall, recv_ref, wide_ref)).T.astype(BF)
    cuts = column_cuts(leaf)
    y_t = []
    for low, high, _ in cuts:
        total = None
        for left, right, base in cuts:
            if left <= low:
                rows = slice(base + low - left, base + high - left)
                term = dot(owned[:, left:right], packed_ref[rows, 0 : right - left], NT)
                total = term if total is None else total + term
        y_t.append(total)
    y_ref[...] = jnp.concatenate(y_t, axis=1).astype(BF)


def backward_kernel(y_ref, packed_ref, out_ref):
    leaf = out_ref.shape[0]
    cuts = column_cuts(leaf)
    y_t = y_ref[...]
    bare_t = [
        dot(y_t[:, low:], packed_ref[base : base + leaf - low, 0 : high - low])
        for low, high, base in cuts
    ]
    out_ref[...] = jnp.concatenate(bare_t, axis=1).T


def hot_at(where, rows):
    cols = where.shape[1]
    here = row_ids(rows, cols).astype(F32).astype(BF)
    there = jnp.broadcast_to(where, (SUB, cols)).astype(BF)
    there = jnp.concatenate([there] * (rows // SUB), axis=0)
    return jnp.where(here == there, jnp.ones((rows, cols), BF), jnp.zeros((rows, cols), BF))


def turn(value, shift):
    shift = shift % 128
    return pltpu.roll(value, shift, 1) if shift else value


def tree_kernel(
    front_ref, got_ref, other_ref, bare_hbm, out_ref,
    e0_ref, e1_ref, e2_ref, a01_ref, a02_ref, a12_ref, spots_ref,
):
    front = front_ref[0]
    first = front == 0
    sides = (got_ref, other_ref)
    lane = lane_ids(32, 128)
    none = jnp.zeros((32, 128), BF)
    for peer in range(TREE):
        rows = slice(peer * 32, (peer + 1) * 32)
        mine = got_ref[peer, 32:64, :].astype(F32)
        theirs = other_ref[peer, 32:64, :].astype(F32)
        left = jnp.where(first, mine, theirs)
        right = jnp.where(first, theirs, mine)
        e2_ref[rows, 0:128] = left[:, 0:128].astype(BF)
        e2_ref[rows, 128:256] = right[:, 0:128].astype(BF)
        left, right = left[:, 128:256], right[:, 128:256]
        low1 = jnp.where(lane < 64, left, turn(right, 64))
        inside = (lane >= 64) & (lane < 96)
        to = ((peer // 2) % 2) * 64
        low0 = turn(jnp.where(inside, left, 0.0), to - 64)
        low0 = low0 + turn(jnp.where(inside, right, 0.0), to + 32 - 64)
        tile = peer // 4
        for ref, low in ((e1_ref, low1), (e0_ref, low0)):
            ref[rows, tile * 128 : (tile + 1) * 128] = low.astype(BF)
            ref[rows, (1 - tile) * 128 : (2 - tile) * 128] = none
    for side, table in enumerate(sides):
        for peer in range(TREE):
            at = peer * 2 * SUB + (front ^ side) * SUB
            rows = pl.ds(pl.multiple_of(at, SUB), SUB)
            for pair, ref in enumerate((a01_ref, a02_ref, a12_ref)):
                where = table[peer, 64 + pair : 65 + pair, 192:256].astype(F32)
                if pair == 0:
                    where = where + float(peer // 4 * 128)
                flipped = table[peer, 64:80, pair * 64 : (pair + 1) * 64]
                ref[rows, :] = dot(flipped, hot_at(where, 256), NT).astype(BF)
    for level in range(3):
        for quad in range(4):
            parts = []
            for peer in range(quad % 2 * 4, quad % 2 * 4 + 4):
                where = sides[quad // 2][peer, 67 + level : 68 + level, 192:256].astype(F32)
                parts.append(where + (peer // 2 * 64.0, peer // 4 * 128.0, 0.0)[level])
            spots_ref[level * 4 + quad] = hot_at(jnp.concatenate(parts, axis=1), 256)
    lane = lane_ids(COLS, 128)
    half = lane < 64
    sums = []
    for level in range(3):
        begin = 64 + level * SUB
        inside = (lane >= begin) & (lane < begin + SUB)
        tiles = []
        for tile in range(2):
            totals = []
            for table in sides:
                total = jnp.zeros((COLS, 128), F32)
                for at in range(4):
                    piece = table[tile * 4 + at, 0:32, 128:256].astype(F32)
                    total = total + turn(jnp.where(inside, piece, 0.0), at * 32 - begin)
                totals.append(total)
            mine, theirs = totals
            left = jnp.where(first, mine, theirs)
            right = jnp.where(first, theirs, mine)
            tiles.append(left + turn(right, SUB))
        rest = jnp.concatenate(tiles, axis=1)
        tile = slice(level // 2 * 128, level // 2 * 128 + 128)
        for quad in range(4):
            table = sides[quad // 2]
            halves = []
            for pair in range(2):
                peer = quad % 2 * 4 + pair * 2
                left = table[peer, 0:32, tile].astype(F32)
                right = table[peer + 1, 0:32, tile].astype(F32)
                if level == 1:
                    halves.append(jnp.where(half, turn(left, 64), right))
                else:
                    halves.append(jnp.where(half, left, turn(right, 64)))
            moved = jnp.concatenate(halves, axis=1).astype(BF)
            rest = rest - dot(moved, spots_ref[level * 4 + quad], NT)
        sums.append(rest)
    r0, r1, r2 = sums
    e0, e1, e2 = e0_ref[...], e1_ref[...], e2_ref[...]
    a01, a02, a12 = a01_ref[...], a02_ref[...], a12_ref[...]
    c01 = dot(e0, a01, TN).astype(BF)
    c02 = dot(e0, a02, TN).astype(BF)
    c12 = dot(e1, a12, TN).astype(BF)
    g0 = dot(e0, e0, TN).astype(BF)
    g1 = dot(e1, e1, TN).astype(BF)
    g2 = dot(e2, e2, TN).astype(BF)
    r0 = r0.astype(BF)
    r1 = (r1 - dot(r0, c01)).astype(BF)
    r2 = (r2 - dot(r0, c02) - dot(r1, c12)).astype(BF)
    x2 = dot(r2, g2).astype(BF)
    x1 = (dot(r1, g1) - dot(x2, c12, NT)).astype(BF)
    x0 = (dot(r0, g0) - dot(x2, c02, NT) - dot(x1, c01, NT)).astype(BF)
    solved = (x0, x1, x2)
    own = []
    for level in range(3):
        for tile in range(2):
            piece = solved[level][:, tile * 128 : (tile + 1) * 128].astype(F32)
            own.append(jnp.where(first, piece, turn(piece, -SUB)))
    for quad in range(2):
        picks = [dot(solved[level], spots_ref[level * 4 + quad]) for level in range(3)]
        for at in range(4):
            peer = quad * 4 + at
            part = slice(at // 2 * 128, at // 2 * 128 + 128)
            p0, p1, p2 = [pick[:, part] for pick in picks]
            if at % 2:
                p0, p2 = turn(p0, 64), turn(p2, 64)
            else:
                p1 = turn(p1, 64)
            out_ref[peer, :, 0:128] = jnp.where(half, p0, p1).astype(BF)
            rest = jnp.where(half, p2, 0.0)
            for level in range(3):
                begin = 64 + level * SUB
                piece = turn(own[level * 2 + quad], begin - at * 32)
                rest = jnp.where((lane >= begin) & (lane < begin + SUB), piece, rest)
            out_ref[peer, :, 128:256] = rest.astype(BF)


def finish_kernel(got_ref, back_ref, leaf_ref, out_ref, sep_ref):
    table = got_ref[...].reshape(256, 256)
    out_ref[...] = leaf_ref[...] - dot(back_ref[...], table, NT)
    pick = hot(lane_ids(48, 256) == row_ids(48, 256) + 192)
    rows = dot(pick, table, NT).astype(BF)
    for level in range(3):
        sep_ref[level] = rows[level * SUB : (level + 1) * SUB, :]


def on_device(
    rhs_parts,
    send_order,
    recv_place,
    sep_rhs,
    leaf_inv,
    leaf_panels,
    leaf_rows,
    sep_inv,
    sep_panels,
    sep_rows,
):
    owners = lax.axis_size("tree") * lax.axis_size("peer")
    rhs = rhs_parts[0, 0]
    leaf, width = rhs.shape
    inv = leaf_inv[0, 0]
    panels = leaf_panels[0, 0].reshape(-1, leaf)
    keep = leaf // owners
    half = width // 2
    tall = 2 * keep
    span = -(-keep // 8) * 8
    slots = owners * span
    wide = pltpu.VMEM((owners * tall + span, half), F32)
    sds = jax.ShapeDtypeStruct

    (sent,) = call(
        lambda *refs: send_kernel(keep, tall, *refs),
        "send_rows",
        [HB, HB],
        [(sds((owners * tall, half), BF), HB)],
        [
            pltpu.VMEM((1, leaf), jnp.int32),
            pltpu.VMEM((leaf, width), BF),
            pltpu.VMEM((leaf + 8, width), F32),
            pltpu.VMEM((owners * tall + 8, half), F32),
            pltpu.VMEM((owners * tall, half), BF),
            DMA((3,)),
        ],
        flops=2 * leaf * leaf * width,
        nbytes=2 * leaf * width * 2,
        vmem=VMEM_ALL,
    )(send_order[0], rhs)
    recv = lax.all_to_all(
        sent.reshape(owners, tall // 4, 4, half), ("tree", "peer"), split_axis=0, concat_axis=0, tiled=True
    ).reshape(owners * tall, half)

    place = jnp.pad(
        recv_place[0, 0].reshape(owners, keep), ((0, 0), (0, span - keep)), constant_values=-1
    ).reshape(1, slots)
    span = jnp.swapaxes(sep_panels[0, 0], 1, 2)
    packed_rows = sum(leaf - low for low, _, _ in column_cuts(leaf))
    push, back, side, packed = call(
        factor_kernel,
        "factor_products",
        [VM, VM, VM, VM, HB, HB, HB, HB],
        [
            (sds((320, slots), BF), VM),
            (sds((leaf, 256), BF), VM),
            (sds((112, 256), BF), VM),
            (sds((packed_rows, 256), BF), HB),
        ],
        [
            pltpu.VMEM(panels.shape, BF),
            pltpu.VMEM(sep_inv.shape[2:], BF),
            pltpu.VMEM(span.shape, BF),
            pltpu.VMEM(sep_rhs.shape[2:], BF),
            DMA((4 + len(column_cuts(leaf)),)),
        ],
        flops=2 * 192 * leaf * (leaf + slots),
        nbytes=2 * leaf * leaf + 2 * 192 * slots + 2 * 256 * leaf,
    )(
        place,
        leaf_rows[0, 0][:, None, :],
        sep_rows[0, 0][:, None, :],
        inv,
        panels,
        sep_inv[0, 0],
        span,
        sep_rhs[0, 0],
    )
    (chunks,) = call(
        lambda *refs: push_kernel(keep, tall, *refs),
        "push_updates",
        [VM, VM, VM],
        [(sds((TREE, 80, 256), BF), VM)],
        [wide],
        flops=2 * 192 * slots * width,
        nbytes=2 * slots * (192 + width) + TREE * 80 * 512,
    )(recv, push, side)
    got = lax.all_to_all(chunks, "peer", split_axis=0, concat_axis=0, tiled=True)
    (leaf_y,) = call(
        lambda *refs: forward_kernel(leaf, keep, tall, *refs),
        "leaf_forward",
        [VM, VM, VM],
        [(sds((width, leaf), BF), VM)],
        [wide],
        flops=2 * leaf * width * (leaf + slots),
        nbytes=2 * leaf * leaf + 4 * slots * width,
    )(place, recv, packed)
    got, leaf_y = lax.optimization_barrier((got, leaf_y))
    other = lax.ppermute(got, "front", [(0, 1), (1, 0)])
    front = lax.axis_index("front").astype(jnp.int32).reshape(1)
    (bare,) = call(
        backward_kernel,
        "leaf_backward",
        [VM, VM],
        [(sds((leaf, width), F32), VM)],
        flops=2 * leaf * width * leaf,
        nbytes=2 * leaf * leaf + 6 * leaf * width,
    )(leaf_y, packed)
    square = pltpu.VMEM((256, 256), BF)
    (solved,) = call(
        tree_kernel,
        "separator_tree",
        [SM, VM, VM, pl.BlockSpec(memory_space=pl.ANY)],
        [(sds((TREE, COLS, 256), BF), VM)],
        [square] * 6 + [pltpu.VMEM((12, 256, 256), BF)],
        flops=2 * 32 * 256 * 256 * 30 + 2 * 48 * 16 * 64 * 256,
        nbytes=TREE * 192 * 512,
    )(front, got, other, bare)
    back_got = lax.all_to_all(solved, "peer", split_axis=0, concat_axis=0, tiled=True)

    leaf_solution, sep_solution = call(
        finish_kernel,
        "finish",
        [VM, VM, VM],
        [(sds((leaf, width), F32), VM), (sds((3, SUB, width), BF), VM)],
        flops=2 * leaf * 256 * width,
        nbytes=leaf * width * 8 + leaf * 512 + TREE * COLS * 512,
    )(back_got, back, bare)
    return leaf_solution[None, None], sep_solution[None, None]


def solution(mesh):
    leaves, fronts = mesh.shape["leaf"], mesh.shape["front"]
    grid = Mesh(
        np.asarray(mesh.devices).reshape(leaves // TREE, TREE, fronts), ("tree", "peer", "front")
    )
    leaf = ("tree", "peer")
    in_specs = (
        P(leaf, "front", None, None),
        P(leaf, "front", None),
        P(leaf, "front", None),
        P(leaf, "front", None, None, None),
        P(leaf, "front", None, None),
        P(leaf, "front", None, None, None),
        P(leaf, "front", None, None),
        P(leaf, "front", None, None),
        P(leaf, "front", None, None, None),
        P(leaf, "front", None, None),
    )
    out_specs = (P(leaf, "front", None, None), P(leaf, "front", None, None, None))
    return jax.shard_map(
        on_device, mesh=grid, in_specs=in_specs, out_specs=out_specs, check_vma=False
    )
```

```python
import jax
import jax.numpy as jnp
import numpy as np
from jax import lax
from jax.experimental import pallas as pl
from jax.experimental.pallas import tpu as pltpu
from jax.sharding import Mesh, PartitionSpec as P

BF = jnp.bfloat16
F32 = jnp.float32
SUB = 16
TREE = 8
COLS = 32
VMEM_CAP = 40 * 1024 * 1024
VMEM_ALL = 62 * 1024 * 1024

NN = (((1,), (0,)), ((), ()))
NT = (((1,), (1,)), ((), ()))
TN = (((0,), (0,)), ((), ()))


def dot(a, b, dims=NN):
    return lax.dot_general(a, b, dims, preferred_element_type=F32)


def lane_ids(rows, cols):
    return lax.broadcasted_iota(jnp.int32, (rows, cols), 1)


def row_ids(rows, cols):
    return lax.broadcasted_iota(jnp.int32, (rows, cols), 0)


def hot(mask):
    return jnp.where(mask, 1.0, 0.0).astype(BF)


VM = pl.BlockSpec(memory_space=pltpu.VMEM)
SM = pl.BlockSpec(memory_space=pltpu.SMEM)
HB = pl.BlockSpec(memory_space=pltpu.HBM)
DMA = pltpu.SemaphoreType.DMA


def call(kernel, name, ins, outs, scratch=(), flops=0, nbytes=0, vmem=VMEM_CAP):
    return pl.pallas_call(
        kernel,
        out_shape=[shape for shape, _ in outs],
        in_specs=list(ins),
        out_specs=[spec for _, spec in outs],
        scratch_shapes=list(scratch),
        compiler_params=pltpu.CompilerParams(vmem_limit_bytes=vmem),
        cost_estimate=pl.CostEstimate(flops=flops, bytes_accessed=nbytes, transcendentals=0),
        name=name,
    )


def fetch(source, target, sem):
    copy = pltpu.make_async_copy(source, target, sem)
    copy.start()
    return copy


def send_kernel(
    keep, tall, order_hbm, rhs_hbm, out_hbm, order_ref, rhs_ref, picked_ref, stage_ref, out_ref, sems
):
    rows, width = rhs_ref.shape
    half = width // 2
    order_in = fetch(order_hbm, order_ref, sems.at[0])
    rhs_in = fetch(rhs_hbm, rhs_ref, sems.at[1])
    tail = picked_ref.shape[0] - rows
    picked_ref[rows:, :] = jnp.zeros((tail, width), F32)
    lanes = lane_ids(128, 128).astype(F32).astype(BF)
    one, zero = jnp.ones((128, 128), BF), jnp.zeros((128, 128), BF)
    order_in.wait()
    hots = []
    for at in range(0, rows, 128):
        ids = jnp.broadcast_to(order_ref[:, at : at + 128], (128, 128)).T.astype(F32)
        tiles = [jnp.where(lanes == (ids - base).astype(BF), one, zero) for base in range(0, rows, 128)]
        hots.append(jnp.concatenate(tiles, axis=1))
    rhs_in.wait()
    picked_ref[0:rows, :] = dot(jnp.concatenate(hots, axis=0), rhs_ref[...])
    span = -(-keep // 8) * 8
    for owner in range(rows // keep):
        source = slice(owner * keep, owner * keep + span)
        base = owner * tall
        stage_ref[base : base + span, :] = picked_ref[source, 0:half]
        stage_ref[base + keep : base + keep + span, :] = picked_ref[source, half:width]
    out_ref[...] = stage_ref[0 : out_ref.shape[0], :].astype(BF)
    fetch(out_ref, out_hbm, sems.at[2]).wait()


def side_by_side(keep, tall, recv_ref, wide_ref):
    sent = recv_ref.shape[0]
    span = wide_ref.shape[0] - sent
    wide_ref[0:sent, :] = recv_ref[...].astype(F32)
    wide_ref[sent:, :] = jnp.zeros((span, wide_ref.shape[1]), F32)
    rows = []
    for base in range(0, sent, tall):
        left = wide_ref[base : base + span, :]
        right = wide_ref[base + keep : base + keep + span, :]
        rows.append(jnp.concatenate([left, right], axis=1))
    return jnp.concatenate(rows, axis=0).astype(BF)


def column_cuts(leaf):
    cuts, base = [], 0
    for low in range(0, leaf, 256):
        cuts.append((low, min(low + 256, leaf), base))
        base += leaf - low
    return cuts


def factor_kernel(
    place_ref, rows_ref, srow_ref, inv_ref, panels_hbm, sinv_hbm, span_hbm, srhs_hbm,
    push_ref, back_ref, side_ref, packed_hbm, panels_ref, sinv_ref, span_ref, srhs_ref, sems,
):
    moves = [
        fetch(sinv_hbm, sinv_ref, sems.at[0]),
        fetch(span_hbm, span_ref, sems.at[1]),
        fetch(srhs_hbm, srhs_ref, sems.at[2]),
        fetch(panels_hbm, panels_ref, sems.at[3]),
    ]
    leaf = inv_ref.shape[0]
    slots = place_ref.shape[1]
    upd = rows_ref.shape[2]
    cuts = column_cuts(leaf)
    leaving = [
        fetch(
            inv_ref.at[low:leaf, low:high],
            packed_hbm.at[base : base + leaf - low, 0 : high - low],
            sems.at[4 + at],
        )
        for at, (low, high, base) in enumerate(cuts)
    ]
    spread = hot(row_ids(leaf, slots) == place_ref[...])
    for move in moves:
        move.wait()
    product = [dot(panels_ref[:, low:], inv_ref[low:, low:high]) for low, high, _ in cuts]
    product = jnp.concatenate(product, axis=1)
    push_ref[0:192, :] = dot(product.astype(BF), spread).astype(BF)
    padded = jnp.concatenate([product, jnp.zeros((256 - product.shape[0], leaf), F32)], axis=0)
    back_ref[...] = padded.astype(BF).T
    cols = sinv_ref.shape[1]
    lane = lane_ids(cols, 256)
    source = jnp.where(
        lane < 128, lane + 96, jnp.where(lane < 192, lane - 96, jnp.where(lane < 224, lane - 192, -1))
    )
    side_ref[0:32, :] = dot(sinv_ref[...], hot(row_ids(cols, 256) == source)).astype(BF)
    lists = [srow_ref[pair].astype(F32) for pair in range(3)]
    lists += [rows_ref[level].astype(F32) for level in range(3)]
    lists = jnp.concatenate(lists + [jnp.zeros((SUB - 6, upd), F32)], axis=0)
    flipped = [span_ref[pair].astype(F32) for pair in range(3)]
    side_ref[32:48, :] = jnp.concatenate(flipped + [lists], axis=1).astype(BF)
    for level in range(3):
        side_ref[48 + level * SUB : 64 + level * SUB, :] = srhs_ref[level]
    side_ref[96:112, :] = jnp.zeros((SUB, 256), BF)
    for copy in leaving:
        copy.wait()


def push_kernel(keep, tall, recv_ref, push_ref, side_ref, out_ref, wide_ref):
    sums = dot(push_ref[0:192, :], side_by_side(keep, tall, recv_ref, wide_ref))
    rows = jnp.concatenate([sums, side_ref[48:112, :].astype(F32)], axis=0)
    turned = rows.astype(BF).T
    meta = side_ref[0:48, :]
    for peer in range(TREE):
        out_ref[peer, 0:32, :] = turned[peer * COLS : (peer + 1) * COLS, :]
        out_ref[peer, 32:80, :] = meta


def forward_kernel(leaf, keep, tall, place_ref, recv_ref, packed_ref, y_ref, wide_ref):
    slots = place_ref.shape[1]
    spread = hot(row_ids(leaf, slots) == place_ref[...])
    owned = dot(spread, side_by_side(keep, tall, recv_ref, wide_ref)).astype(BF).T
    cuts = column_cuts(leaf)
    y_t = []
    for low, high, _ in cuts:
        total = None
        for left, right, base in cuts:
            if left <= low:
                rows = slice(base + low - left, base + high - left)
                term = dot(owned[:, left:right], packed_ref[rows, 0 : right - left], NT)
                total = term if total is None else total + term
        y_t.append(total)
    y_ref[...] = jnp.concatenate(y_t, axis=1).astype(BF)


def backward_kernel(y_ref, packed_ref, out_ref):
    leaf = out_ref.shape[0]
    cuts = column_cuts(leaf)
    y_t = y_ref[...]
    bare_t = [
        dot(y_t[:, low:], packed_ref[base : base + leaf - low, 0 : high - low])
        for low, high, base in cuts
    ]
    out_ref[...] = jnp.concatenate(bare_t, axis=1).T


def hot_at(where, rows):
    cols = where.shape[1]
    here = row_ids(rows, cols).astype(F32).astype(BF)
    there = jnp.broadcast_to(where, (SUB, cols)).astype(BF)
    there = jnp.concatenate([there] * (rows // SUB), axis=0)
    return jnp.where(here == there, jnp.ones((rows, cols), BF), jnp.zeros((rows, cols), BF))


def turn(value, shift):
    shift = shift % 128
    return pltpu.roll(value, shift, 1) if shift else value


def tree_kernel(
    front_ref, got_ref, other_ref, bare_hbm, out_ref,
    e0_ref, e1_ref, e2_ref, a01_ref, a02_ref, a12_ref, spots_ref,
):
    front = front_ref[0]
    first = front == 0
    sides = (got_ref, other_ref)
    lane = lane_ids(32, 128)
    none = jnp.zeros((32, 128), BF)
    for peer in range(TREE):
        rows = slice(peer * 32, (peer + 1) * 32)
        mine = got_ref[peer, 32:64, :].astype(F32)
        theirs = other_ref[peer, 32:64, :].astype(F32)
        left = jnp.where(first, mine, theirs)
        right = jnp.where(first, theirs, mine)
        e2_ref[rows, 0:128] = left[:, 0:128].astype(BF)
        e2_ref[rows, 128:256] = right[:, 0:128].astype(BF)
        left, right = left[:, 128:256], right[:, 128:256]
        low1 = jnp.where(lane < 64, left, turn(right, 64))
        inside = (lane >= 64) & (lane < 96)
        to = ((peer // 2) % 2) * 64
        low0 = turn(jnp.where(inside, left, 0.0), to - 64)
        low0 = low0 + turn(jnp.where(inside, right, 0.0), to + 32 - 64)
        tile = peer // 4
        for ref, low in ((e1_ref, low1), (e0_ref, low0)):
            ref[rows, tile * 128 : (tile + 1) * 128] = low.astype(BF)
            ref[rows, (1 - tile) * 128 : (2 - tile) * 128] = none
    for side, table in enumerate(sides):
        for peer in range(TREE):
            at = peer * 2 * SUB + (front ^ side) * SUB
            rows = pl.ds(pl.multiple_of(at, SUB), SUB)
            for pair, ref in enumerate((a01_ref, a02_ref, a12_ref)):
                where = table[peer, 64 + pair : 65 + pair, 192:256].astype(F32)
                if pair == 0:
                    where = where + float(peer // 4 * 128)
                flipped = table[peer, 64:80, pair * 64 : (pair + 1) * 64]
                ref[rows, :] = dot(flipped, hot_at(where, 256), NT).astype(BF)
    for level in range(3):
        for quad in range(4):
            parts = []
            for peer in range(quad % 2 * 4, quad % 2 * 4 + 4):
                where = sides[quad // 2][peer, 67 + level : 68 + level, 192:256].astype(F32)
                parts.append(where + (peer // 2 * 64.0, peer // 4 * 128.0, 0.0)[level])
            spots_ref[level * 4 + quad] = hot_at(jnp.concatenate(parts, axis=1), 256)
    lane = lane_ids(COLS, 128)
    half = lane < 64
    sums = []
    for level in range(3):
        begin = 64 + level * SUB
        inside = (lane >= begin) & (lane < begin + SUB)
        tiles = []
        for tile in range(2):
            totals = []
            for table in sides:
                total = jnp.zeros((COLS, 128), F32)
                for at in range(4):
                    piece = table[tile * 4 + at, 0:32, 128:256].astype(F32)
                    total = total + turn(jnp.where(inside, piece, 0.0), at * 32 - begin)
                totals.append(total)
            mine, theirs = totals
            left = jnp.where(first, mine, theirs)
            right = jnp.where(first, theirs, mine)
            tiles.append(left + turn(right, SUB))
        rest = jnp.concatenate(tiles, axis=1)
        tile = slice(level // 2 * 128, level // 2 * 128 + 128)
        for quad in range(4):
            table = sides[quad // 2]
            halves = []
            for pair in range(2):
                peer = quad % 2 * 4 + pair * 2
                left = table[peer, 0:32, tile].astype(F32)
                right = table[peer + 1, 0:32, tile].astype(F32)
                if level == 1:
                    halves.append(jnp.where(half, turn(left, 64), right))
                else:
                    halves.append(jnp.where(half, left, turn(right, 64)))
            moved = jnp.concatenate(halves, axis=1).astype(BF)
            rest = rest - dot(moved, spots_ref[level * 4 + quad], NT)
        sums.append(rest)
    r0, r1, r2 = sums
    e0, e1, e2 = e0_ref[...], e1_ref[...], e2_ref[...]
    a01, a02, a12 = a01_ref[...], a02_ref[...], a12_ref[...]
    c01 = dot(e0, a01, TN).astype(BF)
    c02 = dot(e0, a02, TN).astype(BF)
    c12 = dot(e1, a12, TN).astype(BF)
    g0 = dot(e0, e0, TN).astype(BF)
    g1 = dot(e1, e1, TN).astype(BF)
    g2 = dot(e2, e2, TN).astype(BF)
    r0 = r0.astype(BF)
    r1 = (r1 - dot(r0, c01)).astype(BF)
    r2 = (r2 - dot(r0, c02) - dot(r1, c12)).astype(BF)
    x2 = dot(r2, g2).astype(BF)
    x1 = (dot(r1, g1) - dot(x2, c12, NT)).astype(BF)
    x0 = (dot(r0, g0) - dot(x2, c02, NT) - dot(x1, c01, NT)).astype(BF)
    solved = (x0, x1, x2)
    own = []
    for level in range(3):
        for tile in range(2):
            piece = solved[level][:, tile * 128 : (tile + 1) * 128].astype(F32)
            own.append(jnp.where(first, piece, turn(piece, -SUB)))
    for quad in range(2):
        picks = [dot(solved[level], spots_ref[level * 4 + quad]) for level in range(3)]
        for at in range(4):
            peer = quad * 4 + at
            part = slice(at // 2 * 128, at // 2 * 128 + 128)
            p0, p1, p2 = [pick[:, part] for pick in picks]
            if at % 2:
                p0, p2 = turn(p0, 64), turn(p2, 64)
            else:
                p1 = turn(p1, 64)
            out_ref[peer, :, 0:128] = jnp.where(half, p0, p1).astype(BF)
            rest = jnp.where(half, p2, 0.0)
            for level in range(3):
                begin = 64 + level * SUB
                piece = turn(own[level * 2 + quad], begin - at * 32)
                rest = jnp.where((lane >= begin) & (lane < begin + SUB), piece, rest)
            out_ref[peer, :, 128:256] = rest.astype(BF)


def finish_kernel(got_ref, back_ref, leaf_ref, out_ref, sep_ref):
    table = got_ref[...].reshape(256, 256)
    out_ref[...] = leaf_ref[...] - dot(back_ref[...], table, NT)
    pick = hot(lane_ids(48, 256) == row_ids(48, 256) + 192)
    rows = dot(pick, table, NT).astype(BF)
    for level in range(3):
        sep_ref[level] = rows[level * SUB : (level + 1) * SUB, :]


def on_device(
    rhs_parts,
    send_order,
    recv_place,
    sep_rhs,
    leaf_inv,
    leaf_panels,
    leaf_rows,
    sep_inv,
    sep_panels,
    sep_rows,
):
    owners = lax.axis_size("tree") * lax.axis_size("peer")
    rhs = rhs_parts[0, 0]
    leaf, width = rhs.shape
    inv = leaf_inv[0, 0]
    panels = leaf_panels[0, 0].reshape(-1, leaf)
    keep = leaf // owners
    half = width // 2
    tall = 2 * keep
    span = -(-keep // 8) * 8
    slots = owners * span
    wide = pltpu.VMEM((owners * tall + span, half), F32)
    sds = jax.ShapeDtypeStruct

    (sent,) = call(
        lambda *refs: send_kernel(keep, tall, *refs),
        "send_rows",
        [HB, HB],
        [(sds((owners * tall, half), BF), HB)],
        [
            pltpu.VMEM((1, leaf), jnp.int32),
            pltpu.VMEM((leaf, width), BF),
            pltpu.VMEM((leaf + 8, width), F32),
            pltpu.VMEM((owners * tall + 8, half), F32),
            pltpu.VMEM((owners * tall, half), BF),
            DMA((3,)),
        ],
        flops=2 * leaf * leaf * width,
        nbytes=2 * leaf * width * 2,
        vmem=VMEM_ALL,
    )(send_order[0], rhs)
    recv = lax.all_to_all(
        sent.reshape(owners, tall // 4, 4, half), ("tree", "peer"), split_axis=0, concat_axis=0, tiled=True
    ).reshape(owners * tall, half)

    place = jnp.pad(
        recv_place[0, 0].reshape(owners, keep), ((0, 0), (0, span - keep)), constant_values=-1
    ).reshape(1, slots)
    span = jnp.swapaxes(sep_panels[0, 0], 1, 2)
    packed_rows = sum(leaf - low for low, _, _ in column_cuts(leaf))
    push, back, side, packed = call(
        factor_kernel,
        "factor_products",
        [VM, VM, VM, VM, HB, HB, HB, HB],
        [
            (sds((320, slots), BF), VM),
            (sds((leaf, 256), BF), VM),
            (sds((112, 256), BF), VM),
            (sds((packed_rows, 256), BF), HB),
        ],
        [
            pltpu.VMEM(panels.shape, BF),
            pltpu.VMEM(sep_inv.shape[2:], BF),
            pltpu.VMEM(span.shape, BF),
            pltpu.VMEM(sep_rhs.shape[2:], BF),
            DMA((4 + len(column_cuts(leaf)),)),
        ],
        flops=2 * 192 * leaf * (leaf + slots),
        nbytes=2 * leaf * leaf + 2 * 192 * slots + 2 * 256 * leaf,
    )(
        place,
        leaf_rows[0, 0][:, None, :],
        sep_rows[0, 0][:, None, :],
        inv,
        panels,
        sep_inv[0, 0],
        span,
        sep_rhs[0, 0],
    )
    (chunks,) = call(
        lambda *refs: push_kernel(keep, tall, *refs),
        "push_updates",
        [VM, VM, VM],
        [(sds((TREE, 80, 256), BF), VM)],
        [wide],
        flops=2 * 192 * slots * width,
        nbytes=2 * slots * (192 + width) + TREE * 80 * 512,
    )(recv, push, side)
    got = lax.all_to_all(chunks, "peer", split_axis=0, concat_axis=0, tiled=True)
    (leaf_y,) = call(
        lambda *refs: forward_kernel(leaf, keep, tall, *refs),
        "leaf_forward",
        [VM, VM, VM],
        [(sds((width, leaf), BF), VM)],
        [wide],
        flops=2 * leaf * width * (leaf + slots),
        nbytes=2 * leaf * leaf + 4 * slots * width,
    )(place, recv, packed)
    got, leaf_y = lax.optimization_barrier((got, leaf_y))
    other = lax.ppermute(got, "front", [(0, 1), (1, 0)])
    front = lax.axis_index("front").astype(jnp.int32).reshape(1)
    (bare,) = call(
        backward_kernel,
        "leaf_backward",
        [VM, VM],
        [(sds((leaf, width), F32), VM)],
        flops=2 * leaf * width * leaf,
        nbytes=2 * leaf * leaf + 6 * leaf * width,
    )(leaf_y, packed)
    square = pltpu.VMEM((256, 256), BF)
    (solved,) = call(
        tree_kernel,
        "separator_tree",
        [SM, VM, VM, pl.BlockSpec(memory_space=pl.ANY)],
        [(sds((TREE, COLS, 256), BF), VM)],
        [square] * 6 + [pltpu.VMEM((12, 256, 256), BF)],
        flops=2 * 32 * 256 * 256 * 30 + 2 * 48 * 16 * 64 * 256,
        nbytes=TREE * 192 * 512,
    )(front, got, other, bare)
    back_got = lax.all_to_all(solved, "peer", split_axis=0, concat_axis=0, tiled=True)

    leaf_solution, sep_solution = call(
        finish_kernel,
        "finish",
        [VM, VM, VM],
        [(sds((leaf, width), F32), VM), (sds((3, SUB, width), BF), VM)],
        flops=2 * leaf * 256 * width,
        nbytes=leaf * width * 8 + leaf * 512 + TREE * COLS * 512,
    )(back_got, back, bare)
    return leaf_solution[None, None], sep_solution[None, None]


def solution(mesh):
    leaves, fronts = mesh.shape["leaf"], mesh.shape["front"]
    grid = Mesh(
        np.asarray(mesh.devices).reshape(leaves // TREE, TREE, fronts), ("tree", "peer", "front")
    )
    leaf = ("tree", "peer")
    in_specs = (
        P(leaf, "front", None, None),
        P(leaf, "front", None),
        P(leaf, "front", None),
        P(leaf, "front", None, None, None),
        P(leaf, "front", None, None),
        P(leaf, "front", None, None, None),
        P(leaf, "front", None, None),
        P(leaf, "front", None, None),
        P(leaf, "front", None, None, None),
        P(leaf, "front", None, None),
    )
    out_specs = (P(leaf, "front", None, None), P(leaf, "front", None, None, None))
    return jax.shard_map(
        on_device, mesh=grid, in_specs=in_specs, out_specs=out_specs, check_vma=False
    )
```
